256 devices in a mesh: layer: 4 (over z_hi, core), grid: 64 (over z_lo, y, x).
Axes of the slice: x: 4, y: 4, z: 8 (z_hi: 2, z_lo: 4; z = z_hi * 4 + z_lo), core: 2. Of those that a mesh axis runs over, the one named last changes fastest.
Arguments:
- band_blocks: bfloat16 [640, 9, 128, 128], P('grid'), may hold values from -7 to 7, as said below
- retained: int32 [640, 9], P('grid'), may hold values from 0 to 1, as said below
Outputs:
- purified: bfloat16 [640, 9, 128, 128], P('grid', None, 'layer')
The draws below stay inside these ranges and needn't reach their ends.
Inputs may be any that keep to these rules, and one draw needn't show every extreme that they name: `band_blocks`: the matrix is symmetric: block slot w of block row i equals the transpose of block slot 8 - w of block row (i + w - 4) mod 640. retained[i, w] = 1 exactly when retained[(i + w - 4) mod 640, 8 - w] = 1; the middle slot w = 4 is 1 in every block row.
All inputs are finite; a program needn't handle non-finite values.
Results may differ from the reference program's by a relative error of at most 0.005.
Values may be sent and summed in bfloat16 or wider, within the bound.
No kernel may reach another device: no remote copies, remote signals or barrier semaphores. Data moves between devices by JAX's collectives and lax.ppermute only.
A program may use at most 64 MiB of HBM per device.

```python
import jax
import jax.numpy as jnp
from jax import lax

BLOCK = 128
REACH = 4
BAND = 9
STEPS = 2
NB = 640


def mirror_tables():
    row_table = (jnp.arange(NB)[:, None] + jnp.arange(BAND)[None, :] - REACH) % NB
    slot_table = (BAND - 1 - jnp.arange(BAND))[None, :]
    return (row_table.astype(jnp.int32), slot_table.astype(jnp.int32))


def draw_band_blocks(key, part):
    first_key = jax.random.fold_in(key, 11)
    second_key = jax.random.fold_in(key, 12)
    shape = (NB, BAND, BLOCK, BLOCK)
    base = jnp.clip(jax.random.normal(first_key, shape, jnp.float32), -3.5, 3.5)
    extra = jnp.clip(jax.random.normal(second_key, shape, jnp.float32), -3.5, 3.5)
    row_table, slot_table = mirror_tables()
    mirror = jnp.swapaxes(base[row_table, slot_table], 2, 3)
    extra_mirror = jnp.swapaxes(extra[row_table, slot_table], 2, 3)
    joined = 1.026 * (base + mirror) + 0.57275649 * (extra + extra_mirror)
    return jnp.clip(joined, -7.0, 7.0).astype(jnp.bfloat16)


def draw_retained(key, part):
    coin_key = jax.random.fold_in(key, 21)
    coins = jax.random.randint(coin_key, (NB, BAND), 0, 2).astype(jnp.int32)
    row_table, slot_table = mirror_tables()
    joined = jnp.maximum(coins, coins[row_table, slot_table])
    middle = (jnp.arange(BAND) == REACH)[None, :]
    return jnp.where(middle, 1, joined).astype(jnp.int32)


def setup_inputs(seed: int = 0) -> dict:
    seeds = jax.random.split(jax.random.key(seed), 3)
    return {
        "band_blocks": draw_band_blocks(jax.random.fold_in(seeds[2], 71), 0),
        "retained": draw_retained(jax.random.fold_in(seeds[2], 71), 0),
    }


def band_product(left_blocks, right_blocks):
    left_wide = left_blocks.astype(jnp.float32)
    right_wide = right_blocks.astype(jnp.float32)
    total = jnp.zeros(left_blocks.shape, jnp.float32)
    for offset in range(BAND):
        moved = jnp.roll(right_wide, REACH - offset, axis=0)
        lowest = max(0, offset - REACH)
        highest = min(BAND, BAND + offset - REACH)
        source = moved[:, lowest - offset + REACH:highest - offset + REACH]
        product_term = jnp.einsum('nab,nwbc->nwac', left_wide[:, offset], source, precision=lax.Precision.HIGHEST)
        total = total.at[:, lowest:highest].add(product_term)
    return total


def reference(band_blocks, retained):
    kept = (retained != 0)[:, :, None, None]
    current = jnp.where(kept, band_blocks, jnp.zeros_like(band_blocks))
    for repeat in range(STEPS):
        square = jnp.where(kept, band_product(current, current), 0.0).astype(jnp.bfloat16)
        cube = jnp.where(kept, band_product(square, current), 0.0)
        current = ((3.0 * current.astype(jnp.float32) - cube / (4.0 * BAND * BLOCK)) * 0.5).astype(jnp.bfloat16)
    return current
```

```python
import jax
import jax.numpy as jnp
from jax import lax
from jax.experimental import pallas as pl
from jax.experimental.pallas import tpu as pltpu
from jax.sharding import PartitionSpec as P

B = 128
T = 256
R = 10
W = 9
SHARE = 32
SCALE = 1.0 / (4.0 * W * B)
BF = jnp.bfloat16
F32 = jnp.float32

HALO = [(h, c) for h in range(8) for c in range(max(0, h - 4), h + 1)]
HALO_AT = {hc: n for n, hc in enumerate(HALO)}
NH = len(HALO)

ANY = pl.BlockSpec(memory_space=pl.ANY)
VM = pl.BlockSpec(memory_space=pltpu.VMEM)
SM = pl.BlockSpec(memory_space=pltpu.SMEM)


def nt(a, b):
    return lax.dot_general(a, b, (((1,), (1,)), ((), ())), preferred_element_type=F32)


def nn(a, b):
    return lax.dot_general(a, b, (((1,), (0,)), ((), ())), preferred_element_type=F32)


def flip_core():
    return lax.rem(lax.axis_index("layer"), 2)


def own_mask(ret, flip, i, j):
    if not 0 <= i < R:
        i, j = j, i
    w = j - i + 4
    row = jnp.where(flip == 1, R - 1 - i, i)
    slot = jnp.where(flip == 1, W - 1 - w, w)
    return (ret[row, slot] != 0).astype(F32)


def eye():
    r = lax.broadcasted_iota(jnp.int32, (T, T), 0)
    c = lax.broadcasted_iota(jnp.int32, (T, T), 1)
    return (r == c).astype(F32).astype(BF)


def quads(tile, I, J, mask):
    for a in range(2):
        for b in range(2):
            i, j = 2 * I + a, 2 * J + b
            q = tile[a * B : (a + 1) * B, b * B : (b + 1) * B]
            yield a, b, (q * mask(i, j) if abs(i - j) <= 4 else None)


def put_masked(store, tile, I, J, mask):
    for a, b, q in quads(tile, I, J, mask):
        store(a, b, jnp.zeros((B, B), BF) if q is None else q.astype(BF))


def put_step(store, x, cube, I, J, mask):
    for a, b, q in quads(cube, I, J, mask):
        if q is None:
            store(a, b, jnp.zeros((B, B), BF))
        else:
            xq = x[a * B : (a + 1) * B, b * B : (b + 1) * B].astype(F32)
            store(a, b, ((3.0 * xq - q * SCALE) * 0.5).astype(BF))


def at(ref, *lead):
    def store(a, b, v):
        ref[(*lead, pl.ds(a * B, B), pl.ds(b * B, B))] = v

    return store


def payload_kernel(x, ret, out, buf, sem):
    flip = flip_core()
    copies = []
    for n, (h, c) in enumerate(HALO):
        i, w = h + 2, c - h + 4
        row = jnp.where(flip == 1, R - 1 - i, i)
        slot = jnp.where(flip == 1, W - 1 - w, w)
        cp = pltpu.make_async_copy(x.at[row, slot], buf.at[n], sem.at[n])
        cp.start()
        copies.append(cp)
    for n, (h, c) in enumerate(HALO):
        m = own_mask(ret, flip, h + 2, c + 2)
        out[NH, pl.ds(n, 1), :] = jnp.full((1, B), m, F32).astype(BF)
    out[NH, pl.ds(NH, B - NH), :] = jnp.zeros((B - NH, B), BF)
    for n, (h, c) in enumerate(HALO):
        copies[n].wait()
        m = own_mask(ret, flip, h + 2, c + 2)
        out[n] = (buf[n].astype(F32) * m).astype(BF)


def payload(x, ret):
    return pl.pallas_call(
        payload_kernel,
        out_shape=jax.ShapeDtypeStruct((NH + 1, B, B), BF),
        in_specs=[ANY, SM],
        out_specs=VM,
        scratch_shapes=[pltpu.VMEM((NH, B, B), BF), pltpu.SemaphoreType.DMA((NH,))],
        name="payload",
    )(x, ret)


D1_EARLY = [(0, 2), (2, 0), (1, 2), (2, 1), (2, 2), (1, 3), (3, 1), (2, 3), (3, 2), (2, 4), (4, 2)]
D1_CORNER = [(0, 0), (0, 1), (1, 0), (1, 1)]


def early_kernel(x, ret, xb01, xt, s4, acc, d1, xb, sb):
    flip = flip_core()

    def mask(i, j):
        return own_mask(ret, flip, i, j)

    for I in range(5):
        xb[I, pl.ds(0, B), pl.ds(9 * B, B)] = jnp.zeros((B, B), BF)
        xb[I, pl.ds(B, B), pl.ds(0, B)] = jnp.zeros((B, B), BF)
        for a in range(2):
            for w in range(W):
                i = 2 * I + a
                row = jnp.where(flip == 1, R - 1 - i, i)
                slot = jnp.where(flip == 1, W - 1 - w, w)
                v = x[row, slot].astype(F32) * mask(i, i + w - 4)
                xb[I, pl.ds(a * B, B), pl.ds((a + w) * B, B)] = v.astype(BF)

    def xs(I, lo, hi):
        return xb[I, :, pl.ds((lo - I + 2) * T, (hi - lo + 1) * T)]

    def ss(I, lo, hi):
        return sb[I, :, pl.ds((lo - I + 2) * T, (hi - lo + 1) * T)]

    one = eye()
    xb01[...] = xb[pl.ds(0, 2)]
    for n, (I, K) in enumerate([(0, -2), (0, -1), (1, -1)]):
        xt[n] = nt(one, xs(I, K, K)).astype(BF)

    for I in range(5):
        for J in range(I, min(I + 3, 5)):
            lo, hi = J - 2, I + 2
            s = nt(xs(I, lo, hi), xs(J, lo, hi))

            def store(a, b, v, I=I, J=J):
                sb[I, pl.ds(a * B, B), pl.ds((J - I + 2) * T + b * B, B)] = v

            put_masked(store, s, I, J, mask)
            if J > I:
                sb[J, :, pl.ds((I - J + 2) * T, T)] = nt(one, ss(I, J, J)).astype(BF)

    for n, (I, J) in enumerate(D1_CORNER):
        s4[n] = ss(I, J, J)
        lo, hi = max(0, I - 2, J - 2), min(I, J) + 2
        acc[n] = nt(ss(I, lo, hi), xs(J, lo, hi))

    for I, J in D1_EARLY:
        lo, hi = max(I, J) - 2, min(I, J) + 2
        cube = nt(ss(I, lo, hi), xs(J, lo, hi))

        def store(a, b, v, I=I, J=J):
            d1[J + 2, pl.ds((I - J + 2) * T + a * B, B), pl.ds(b * B, B)] = v

        put_step(store, xs(I, J, J), cube, I, J, mask)


def early(x, ret):
    return pl.pallas_call(
        early_kernel,
        out_shape=[
            jax.ShapeDtypeStruct((2, T, 5 * T), BF),
            jax.ShapeDtypeStruct((3, T, T), BF),
            jax.ShapeDtypeStruct((4, T, T), BF),
            jax.ShapeDtypeStruct((4, T, T), F32),
            jax.ShapeDtypeStruct((7, 5 * T, T), BF),
        ],
        in_specs=[VM, SM],
        out_specs=[VM] * 5,
        scratch_shapes=[pltpu.VMEM((5, T, 5 * T), BF), pltpu.VMEM((5, T, 5 * T), BF)],
        compiler_params=pltpu.CompilerParams(vmem_limit_bytes=40 * 2**20),
        cost_estimate=pl.CostEstimate(flops=2 * 110 * T * T * T, bytes_accessed=12 * 2**20, transcendentals=0),
        name="early",
    )(x, ret)


def halo_mask(ret, flip, hal):
    def mask(i, j):
        if 0 <= i < R or 0 <= j < R:
            return own_mask(ret, flip, i, j)
        h, c = max(i, j) + 8, min(i, j) + 8
        return hal[NH, pl.ds(HALO_AT[h, c], 1), :].astype(F32)

    return mask


def unpack(hal, xh, lowest, one):
    for I in range(lowest, 0):
        for J in range(max(I - 2, lowest), I + 1):
            for a in range(2):
                for b in range(2):
                    h, c = 2 * I + a + 8, 2 * J + b + 8
                    dst = (I + 4, pl.ds(a * B, B), pl.ds((J - I + 2) * T + b * B, B))
                    if abs(h - c) > 4:
                        xh[dst] = jnp.zeros((B, B), BF)
                    elif c <= h:
                        xh[dst] = hal[HALO_AT[h, c]]
                    else:
                        xh[dst] = nt(one[:B, :B], hal[HALO_AT[c, h]]).astype(BF)
            if J < I:
                tile = xh[I + 4, :, pl.ds((J - I + 2) * T, T)]
                xh[J + 4, :, pl.ds((I - J + 2) * T, T)] = nt(one, tile).astype(BF)


def put_cross(xh, xt):
    xh[2, :, pl.ds(4 * T, T)] = xt[0]
    xh[3, :, pl.ds(3 * T, T)] = xt[1]
    xh[3, :, pl.ds(4 * T, T)] = xt[2]


S_CROSS = [(0, -2), (0, -1), (1, -1)]


def corner_kernel(hal, xb01, xt, acc, ret, s3, x1c, xh):
    flip = flip_core()
    mask = halo_mask(ret, flip, hal)
    one = eye()
    unpack(hal, xh, -2, one)
    put_cross(xh, xt)

    def xs(I, lo, hi):
        if I >= 0:
            return xb01[I, :, pl.ds((lo - I + 2) * T, (hi - lo + 1) * T)]
        return xh[I + 4, :, pl.ds((lo - I + 2) * T, (hi - lo + 1) * T)]

    for n, (I, J) in enumerate(S_CROSS):
        lo, hi = I - 2, J + 2
        put_masked(at(s3, n), nt(xs(I, lo, hi), xs(J, lo, hi)), I, J, mask)
    terms = {
        (0, 0): [(0, -2), (1, -1)],
        (0, 1): [(1, -1)],
        (1, 0): [(2, -1)],
        (1, 1): [(2, -1)],
    }
    for n, (I, J) in enumerate(D1_CORNER):
        cube = acc[n]
        for k, m in terms[I, J]:
            cube = cube + nt(s3[k], xs(J, m, m))
        put_step(at(x1c, n), xs(I, J, J), cube, I, J, mask)


def corner(hal, xb01, xt, acc, ret):
    return pl.pallas_call(
        corner_kernel,
        out_shape=[jax.ShapeDtypeStruct((3, T, T), BF), jax.ShapeDtypeStruct((4, T, T), BF)],
        in_specs=[VM, VM, VM, VM, SM],
        out_specs=[VM, VM],
        scratch_shapes=[pltpu.VMEM((4, T, 5 * T), BF)],
        compiler_params=pltpu.CompilerParams(vmem_limit_bytes=24 * 2**20),
        cost_estimate=pl.CostEstimate(flops=2 * 20 * T * T * T, bytes_accessed=4 * 2**20, transcendentals=0),
        name="corner",
    )(hal, xb01, xt, acc, ret)


D1_HALO = [(-2, -2), (-2, -1), (-1, -2), (-1, -1), (-2, 0), (0, -2), (-1, 0), (0, -1), (-1, 1), (1, -1)]


def halo_kernel(hal, xb01, xt, s4, s3, ret, d1_in, d1, xh, sb):
    del d1_in
    flip = flip_core()
    mask = halo_mask(ret, flip, hal)
    one = eye()
    unpack(hal, xh, -4, one)
    put_cross(xh, xt)

    def xs(I, lo, hi):
        if I >= 0:
            return xb01[I, :, pl.ds((lo - I + 2) * T, (hi - lo + 1) * T)]
        return xh[I + 4, :, pl.ds((lo - I + 2) * T, (hi - lo + 1) * T)]

    def spos(I, J):
        return (I + 2, slice(None), pl.ds((J - I + 2) * T, T))

    def ss(I, lo, hi):
        return sb[I + 2, :, pl.ds((lo - I + 2) * T, (hi - lo + 1) * T)]

    for n, (I, J) in enumerate(D1_CORNER):
        sb[spos(I, J)] = s4[n]
    for n, (I, J) in enumerate(S_CROSS):
        sb[spos(I, J)] = s3[n]
        sb[spos(J, I)] = nt(one, s3[n]).astype(BF)
    for I, J in [(-1, -1), (-2, -2), (-1, -2), (-1, -3), (-2, -3), (-2, -4)]:
        lo, hi = I - 2, J + 2
        if I == -2:
            lo = -4
        if J < -2:
            hi = J + 2

        def store(a, b, v, I=I, J=J):
            sb[I + 2, pl.ds(a * B, B), pl.ds((J - I + 2) * T + b * B, B)] = v

        put_masked(store, nt(xs(I, lo, hi), xs(J, lo, hi)), I, J, mask)
    sb[spos(-2, -1)] = nt(one, ss(-1, -2, -2)).astype(BF)

    for I, J in D1_HALO:
        lo, hi = max(I, J) - 2, min(I, J) + 2
        cube = nt(ss(I, lo, hi), xs(J, lo, hi))

        def store(a, b, v, I=I, J=J):
            d1[J + 2, pl.ds((I - J + 2) * T + a * B, B), pl.ds(b * B, B)] = v

        put_step(store, xs(I, J, J), cube, I, J, mask)


def halo(hal, xb01, xt, s4, s3, ret, d1):
    return pl.pallas_call(
        halo_kernel,
        out_shape=jax.ShapeDtypeStruct((7, 5 * T, T), BF),
        in_specs=[VM, VM, VM, VM, VM, SM, VM],
        out_specs=VM,
        scratch_shapes=[pltpu.VMEM((4, T, 5 * T), BF), pltpu.VMEM((4, T, 5 * T), BF)],
        input_output_aliases={6: 0},
        compiler_params=pltpu.CompilerParams(vmem_limit_bytes=32 * 2**20),
        cost_estimate=pl.CostEstimate(flops=2 * 80 * T * T * T, bytes_accessed=9 * 2**20, transcendentals=0),
        name="halo",
    )(hal, xb01, xt, s4, s3, ret, d1)


H = R // 2
Q = 2 * SHARE


def second_kernel(d1_in, x1c, x1p, ret, full, send, d1, left, s1):
    layer = lax.axis_index("layer")
    flip = lax.rem(layer, 2)
    chip_rows = pl.multiple_of(lax.div(layer, 2) * Q, Q)

    for J in range(-2, 5):
        for K in range(max(J - 2, -2), min(J + 2, 4) + 1):
            dst = (J + 2, pl.ds((K - J + 2) * T, T))
            if (K, J) in D1_CORNER:
                d1[dst] = x1c[D1_CORNER.index((K, J))]
            elif (4 - K, 4 - J) in D1_CORNER:
                n = D1_CORNER.index((4 - K, 4 - J))
                for a in range(2):
                    for b in range(2):
                        d1[J + 2, pl.ds((K - J + 2) * T + a * B, B), pl.ds(b * B, B)] = x1p[
                            n, pl.ds((1 - a) * B, B), pl.ds((1 - b) * B, B)
                        ]
            else:
                d1[dst] = d1_in[dst]

    for i in range(H):
        I, a = i // 2, i % 2
        for J in range(-2, 5):
            dst = (pl.ds(i * Q, Q), pl.ds((J + 2) * T, T))
            if abs(I - J) <= 2:
                left[dst] = d1[J + 2, pl.ds((I - J + 2) * T + a * B + chip_rows, Q), :]
            else:
                left[dst] = jnp.zeros((Q, T), BF)

    def mask(i, j):
        return own_mask(ret, flip, i, j)

    def product(lhs, J):
        i0, i1 = max(0, 2 * J - 4), min(H - 1, 2 * J + 5)
        k0, k1 = max(J - 2, -2), min(J + 2, 4)
        a = lhs[pl.ds(i0 * Q, (i1 - i0 + 1) * Q), pl.ds((k0 + 2) * T, (k1 - k0 + 1) * T)]
        return i0, i1, nn(a, d1[J + 2, pl.ds((k0 - J + 2) * T, (k1 - k0 + 1) * T), :])

    for J in range(-2, 5):
        i0, i1, s = product(left, J)
        for i in range(H):
            for b in range(2):
                j = 2 * J + b
                dst = (pl.ds(i * Q, Q), pl.ds((J + 2) * T + b * B, B))
                if abs(i - j) <= 4 and i0 <= i <= i1:
                    q = s[(i - i0) * Q : (i - i0 + 1) * Q, b * B : (b + 1) * B]
                    s1[dst] = (q * mask(i, j)).astype(BF)
                else:
                    s1[dst] = jnp.zeros((Q, B), BF)

    for J in range(-2, 5):
        i0, i1, cube = product(s1, J)
        for i in range(i0, i1 + 1):
            for b in range(2):
                j = 2 * J + b
                if abs(i - j) > 4:
                    continue
                q = cube[(i - i0) * Q : (i - i0 + 1) * Q, b * B : (b + 1) * B] * mask(i, j)
                x = left[pl.ds(i * Q, Q), pl.ds((J + 2) * T + b * B, B)].astype(F32)
                v = ((3.0 * x - q * SCALE) * 0.5).astype(BF)
                w = j - i + 4
                row = jnp.where(flip == 1, R - 1 - i, i)
                near = jnp.where(flip == 1, H - 1 - i, i)
                slot = jnp.where(flip == 1, W - 1 - w, w)
                lo, hi = v[:SHARE], v[SHARE:]
                full[row, slot] = jnp.where(flip == 1, hi, lo)
                send[near, slot] = jnp.where(flip == 1, lo, hi)


def second(d1, x1c, x1p, ret):
    return pl.pallas_call(
        second_kernel,
        out_shape=[
            jax.ShapeDtypeStruct((R, W, SHARE, B), BF),
            jax.ShapeDtypeStruct((H, W, SHARE, B), BF),
        ],
        in_specs=[VM, VM, VM, SM],
        out_specs=[VM, VM],
        scratch_shapes=[
            pltpu.VMEM((7, 5 * T, T), BF),
            pltpu.VMEM((H * Q, 7 * T), BF),
            pltpu.VMEM((H * Q, 7 * T), BF),
        ],
        compiler_params=pltpu.CompilerParams(vmem_limit_bytes=32 * 2**20),
        cost_estimate=pl.CostEstimate(flops=2 * 58 * T * T * T, bytes_accessed=7 * 2**20, transcendentals=0),
        name="second",
    )(d1, x1c, x1p, ret)


def chain(layers, grid):
    pairs = []
    for l in range(layers):
        for g in range(grid):
            t = g + 1 if l % 2 == 0 else g - 1
            k = l if 0 <= t < grid else (l + 2) % layers
            pairs.append((l * grid + g, k * grid + t % grid))
    return pairs


def per_device(x, ret):
    layers, grid = lax.axis_size("layer"), lax.axis_size("grid")
    cores = [(l, l ^ 1) for l in range(layers)]
    flip = lax.rem(lax.axis_index("layer"), 2)
    hal = lax.ppermute(payload(x, ret), ("layer", "grid"), chain(layers, grid))
    xb01, xt, s4, acc, d1 = early(x, ret)
    s3, x1c = corner(hal, xb01, xt, acc, ret)
    x1p = lax.ppermute(x1c, "layer", cores)
    d1 = halo(hal, xb01, xt, s4, s3, ret, d1)
    full, send = second(d1, x1c, x1p, ret)
    other = lax.ppermute(send, "layer", cores)
    return lax.dynamic_update_slice(full, other, (jnp.where(flip == 1, 0, H), 0, 0, 0))


def solution(mesh):
    return jax.shard_map(
        per_device,
        mesh=mesh,
        in_specs=(P("grid", None, None, None), P("grid", None)),
        out_specs=P("grid", None, "layer", None),
        check_vma=False,
    )
```

```python
import jax
import jax.numpy as jnp
from jax import lax
from jax.experimental import pallas as pl
from jax.experimental.pallas import tpu as pltpu
from jax.sharding import PartitionSpec as P

B = 128
T = 256
R = 10
W = 9
SHARE = 32
SCALE = 1.0 / (4.0 * W * B)
BF = jnp.bfloat16
F32 = jnp.float32
MIB = 2**20

A_OFF = [(5, 4), (6, 4), (7, 4), (6, 5), (7, 5), (7, 6)]
A_PACK = [(4, 5), (6, 7)]
A_PAIRS = [(h, c) for h in range(4, 8) for c in range(4, h + 1)]
B_OFF = [(h, c) for h in range(4, 8) for c in range(h - 4, 4)]
C_OFF = [(h - 4, c - 4) for h, c in A_OFF]
C_PACK = [(h - 4, c - 4) for h, c in A_PACK]
MASKS = A_PAIRS + B_OFF
NA = len(A_OFF) + 2
NB = len(B_OFF) + len(C_OFF) + 2
A_ROWS = NA * B + 32
B_ROWS = NB * B + 16

HBM = pl.BlockSpec(memory_space=pltpu.HBM)
VM = pl.BlockSpec(memory_space=pltpu.VMEM)


def nt(a, b):
    return lax.dot_general(a, b, (((1,), (1,)), ((), ())), preferred_element_type=F32)


def nn(a, b):
    return lax.dot_general(a, b, (((1,), (0,)), ((), ())), preferred_element_type=F32)


def flip_core():
    return lax.rem(lax.axis_index("layer"), 2)


def place(flip, i, w):
    return jnp.where(flip == 1, R - 1 - i, i), jnp.where(flip == 1, W - 1 - w, w)


def own_slot(i, j):
    if not 0 <= i < R:
        i, j = j, i
    return i, j - i + 4


def smem_mask(ret, flip, i, j):
    row, slot = place(flip, *own_slot(i, j))
    return (ret[row, slot] != 0).astype(F32)


def iotas(n):
    return lax.broadcasted_iota(jnp.int32, (n, n), 0), lax.broadcasted_iota(jnp.int32, (n, n), 1)


def eye():
    r, c = iotas(T)
    return (r == c).astype(F32).astype(BF)


def whole(row16):
    return jnp.concatenate([row16] * (B // 16), axis=0)


def put_masked(store, tile, I, J, mask):
    for a in range(2):
        for b in range(2):
            i, j = 2 * I + a, 2 * J + b
            if abs(i - j) > 4:
                store(a, b, jnp.zeros((B, B), BF))
            else:
                store(a, b, (tile[a * B : (a + 1) * B, b * B : (b + 1) * B] * mask(i, j)).astype(BF))


def put_step(store, x, cube, I, J, mask):
    for a in range(2):
        for b in range(2):
            i, j = 2 * I + a, 2 * J + b
            if abs(i - j) > 4:
                store(a, b, jnp.zeros((B, B), BF))
            else:
                q = cube[a * B : (a + 1) * B, b * B : (b + 1) * B] * mask(i, j)
                xq = x[a * B : (a + 1) * B, b * B : (b + 1) * B].astype(F32)
                store(a, b, ((3.0 * xq - q * SCALE) * 0.5).astype(BF))


def at(ref, *lead):
    def store(a, b, v):
        ref[(*lead, pl.ds(a * B, B), pl.ds(b * B, B))] = v

    return store


def d1_store(d1, I, J):
    def store(a, b, v):
        d1[J + 2, pl.ds((I - J + 2) * T + a * B, B), pl.ds(b * B, B)] = v

    return store


def pack_kernel(off, packs, masks, x, ret, out, buf, smem, sem, ret_sem):
    flip = flip_core()
    blocks = off + [(h, h) for pair in packs for h in pair]
    load = pltpu.make_async_copy(ret, smem, ret_sem)
    load.start()
    copies = []
    for n, (h, c) in enumerate(blocks):
        row, slot = place(flip, h + 2, c - h + 4)
        cp = pltpu.make_async_copy(x.at[row, slot], buf.at[n], sem.at[n])
        cp.start()
        copies.append(cp)
    load.wait()
    aux = (len(off) + len(packs)) * B
    if masks:
        rows = [jnp.full((1, B), smem_mask(smem, flip, h + 2, c + 2), F32) for h, c in masks]
    else:
        rows = []
    r, c_ = iotas(B)

    def masked(n):
        h, c = blocks[n]
        copies[n].wait()
        m = jnp.full((16, B), smem_mask(smem, flip, h + 2, c + 2), F32).astype(BF)
        return buf[n] * whole(m)

    for n in range(len(off)):
        out[pl.ds(n * B, B), :] = masked(n)
    for k in range(len(packs)):
        n = len(off) + 2 * k
        first, second = masked(n).astype(F32), masked(n + 1).astype(F32)
        out[pl.ds((len(off) + k) * B, B), :] = jnp.where(r <= c_, first, second).astype(BF)
        rows.append(jnp.sum(jnp.where(r == c_, second, 0.0), axis=0, keepdims=True))
    n_rows = out.shape[0] - aux
    rows.append(jnp.zeros((n_rows - len(rows), B), F32))
    out[pl.ds(aux, n_rows), :] = jnp.concatenate(rows, axis=0).astype(BF)


def pack(x, ret, off, packs, masks, rows, name):
    def kernel(*refs):
        pack_kernel(off, packs, masks, *refs)

    n = len(off) + 2 * len(packs)
    return pl.pallas_call(
        kernel,
        out_shape=jax.ShapeDtypeStruct((rows, B), BF),
        in_specs=[HBM, HBM],
        out_specs=VM,
        scratch_shapes=[
            pltpu.VMEM((n, B, B), BF),
            pltpu.SMEM((R, W), jnp.int32),
            pltpu.SemaphoreType.DMA((n,)),
            pltpu.SemaphoreType.DMA,
        ],
        compiler_params=pltpu.CompilerParams(vmem_limit_bytes=4 * MIB),
        cost_estimate=pl.CostEstimate(flops=1000, bytes_accessed=2 * rows * B * 2, transcendentals=0),
        name=name,
    )(x, ret)


D1_EARLY = [(0, 2), (2, 0), (1, 2), (2, 1), (2, 2), (1, 3), (3, 1), (2, 3), (3, 2), (2, 4), (4, 2)]
D1_CORNER = [(0, 0), (0, 1), (1, 0), (1, 1)]
MK = R * W + 6


def early_kernel(x, ret, xb01, xt, s4, acc, d1, mk, xin, xb, sb, smem, sem, ret_sem):
    flip = flip_core()
    load = pltpu.make_async_copy(ret, smem, ret_sem)
    load.start()
    copies = []
    for i in range(R):
        row, _ = place(flip, i, 0)
        cp = pltpu.make_async_copy(x.at[row], xin.at[i], sem.at[i])
        cp.start()
        copies.append(cp)
    load.wait()
    masks = {(i, w): smem_mask(smem, flip, i, i + w - 4) for i in range(R) for w in range(W)}
    for (i, w), m in masks.items():
        mk[pl.ds(i * W + w, 1), :] = jnp.full((1, B), m, F32)
    mk[pl.ds(R * W, MK - R * W), :] = jnp.zeros((MK - R * W, B), F32)

    def mask(i, j):
        return masks[own_slot(i, j)]

    for I in range(5):
        xb[I, pl.ds(0, B), pl.ds(9 * B, B)] = jnp.zeros((B, B), BF)
        xb[I, pl.ds(B, B), pl.ds(0, B)] = jnp.zeros((B, B), BF)
        for a in range(2):
            i = 2 * I + a
            copies[i].wait()
            for w in range(W):
                _, slot = place(flip, i, w)
                m = jnp.full((16, B), masks[i, w], F32).astype(BF)
                xb[I, pl.ds(a * B, B), pl.ds((a + w) * B, B)] = xin[i, slot] * whole(m)

    def xs(I, lo, hi):
        return xb[I, :, pl.ds((lo - I + 2) * T, (hi - lo + 1) * T)]

    def ss(I, lo, hi):
        return sb[I, :, pl.ds((lo - I + 2) * T, (hi - lo + 1) * T)]

    one = eye()
    xb01[...] = xb[pl.ds(0, 2)]
    for n, (I, K) in enumerate([(0, -2), (0, -1), (1, -1)]):
        xt[n] = nt(one, xs(I, K, K)).astype(BF)

    for I in range(5):
        for J in range(I, min(I + 3, 5)):
            lo, hi = J - 2, I + 2
            s = nt(xs(I, lo, hi), xs(J, lo, hi))

            def store(a, b, v, I=I, J=J):
                sb[I, pl.ds(a * B, B), pl.ds((J - I + 2) * T + b * B, B)] = v

            put_masked(store, s, I, J, mask)
            if J > I:
                sb[J, :, pl.ds((I - J + 2) * T, T)] = nt(one, ss(I, J, J)).astype(BF)

    for n, (I, J) in enumerate(D1_CORNER):
        s4[n] = ss(I, J, J)
        lo, hi = max(0, I - 2, J - 2), min(I, J) + 2
        acc[n] = nt(ss(I, lo, hi), xs(J, lo, hi))

    for I, J in D1_EARLY:
        lo, hi = max(I, J) - 2, min(I, J) + 2
        put_step(d1_store(d1, I, J), xs(I, J, J), nt(ss(I, lo, hi), xs(J, lo, hi)), I, J, mask)


def early(x, ret):
    return pl.pallas_call(
        early_kernel,
        out_shape=[
            jax.ShapeDtypeStruct((2, T, 5 * T), BF),
            jax.ShapeDtypeStruct((3, T, T), BF),
            jax.ShapeDtypeStruct((4, T, T), BF),
            jax.ShapeDtypeStruct((4, T, T), F32),
            jax.ShapeDtypeStruct((7, 5 * T, T), BF),
            jax.ShapeDtypeStruct((MK, B), F32),
        ],
        in_specs=[HBM, HBM],
        out_specs=[VM] * 6,
        scratch_shapes=[
            pltpu.VMEM((R, W, B, B), BF),
            pltpu.VMEM((5, T, 5 * T), BF),
            pltpu.VMEM((5, T, 5 * T), BF),
            pltpu.SMEM((R, W), jnp.int32),
            pltpu.SemaphoreType.DMA((R,)),
            pltpu.SemaphoreType.DMA,
        ],
        compiler_params=pltpu.CompilerParams(vmem_limit_bytes=36 * MIB),
        cost_estimate=pl.CostEstimate(flops=2 * 110 * T * T * T, bytes_accessed=12 * MIB, transcendentals=0),
        name="early",
    )(x, ret)


def halo_mask(mk, pa):
    def mask(i, j):
        if 0 <= i < R or 0 <= j < R:
            i, w = own_slot(i, j)
            return mk[pl.ds(i * W + w, 1), :]
        n = MASKS.index((max(i, j) + 8, min(i, j) + 8))
        return pa[pl.ds(NA * B + n, 1), :].astype(F32)

    return mask


def block_of(pa, pb):
    where, packed = {}, {}
    for n, hc in enumerate(A_OFF):
        where[hc] = (pa, n)
    for k, pair in enumerate(A_PACK):
        packed[pair] = (pa, len(A_OFF) + k, NA * B + len(MASKS) + k)
    if pb is not None:
        for n, hc in enumerate(B_OFF + C_OFF):
            where[hc] = (pb, n)
        for k, pair in enumerate(C_PACK):
            packed[pair] = (pb, NB - 2 + k, NB * B + k)
    return where, packed


def unpack(pa, pb, xh, one):
    lowest = -2 if pb is None else -4
    where, packed = block_of(pa, pb)
    r, c_ = iotas(B)

    def dst(h, c):
        I, J = h // 2 - 4, c // 2 - 4
        return (I + 4, pl.ds((h % 2) * B, B), pl.ds((J - I + 2) * T + (c % 2) * B, B))

    for (h, g), (ref, n, row) in packed.items():
        both = ref[pl.ds(n * B, B), :]
        turned = nt(one[:B, :B], both)
        both = both.astype(F32)
        xh[dst(h, h)] = jnp.where(r <= c_, both, turned).astype(BF)
        other = jnp.where(r < c_, turned, both)
        xh[dst(g, g)] = jnp.where(r == c_, ref[pl.ds(row, 1), :].astype(F32), other).astype(BF)
    for I in range(lowest, 0):
        for J in range(max(I - 2, lowest), I + 1):
            for a in range(2):
                for b in range(2):
                    h, c = 2 * I + a + 8, 2 * J + b + 8
                    if h == c:
                        continue
                    if abs(h - c) > 4:
                        xh[dst(h, c)] = jnp.zeros((B, B), BF)
                    elif c < h:
                        ref, n = where[h, c]
                        xh[dst(h, c)] = ref[pl.ds(n * B, B), :]
                    else:
                        ref, n = where[c, h]
                        xh[dst(h, c)] = nt(one[:B, :B], ref[pl.ds(n * B, B), :]).astype(BF)
            if J < I:
                tile = xh[I + 4, :, pl.ds((J - I + 2) * T, T)]
                xh[J + 4, :, pl.ds((I - J + 2) * T, T)] = nt(one, tile).astype(BF)


def put_cross(xh, xt):
    xh[2, :, pl.ds(4 * T, T)] = xt[0]
    xh[3, :, pl.ds(3 * T, T)] = xt[1]
    xh[3, :, pl.ds(4 * T, T)] = xt[2]


def rows_of(xb01, xh):
    def xs(I, lo, hi):
        cols = pl.ds((lo - I + 2) * T, (hi - lo + 1) * T)
        return xb01[I, :, cols] if I >= 0 else xh[I + 4, :, cols]

    return xs


S_CROSS = [(0, -2), (0, -1), (1, -1)]


def corner_kernel(pa, xb01, xt, s4, acc, mk, d1_in, s3, d1, swap, xh):
    del d1_in
    mask = halo_mask(mk, pa)
    one = eye()
    unpack(pa, None, xh, one)
    put_cross(xh, xt)
    xs = rows_of(xb01, xh)

    for n, (I, J) in enumerate(S_CROSS):
        lo, hi = I - 2, J + 2
        put_masked(at(s3, n), nt(xs(I, lo, hi), xs(J, lo, hi)), I, J, mask)
    terms = {
        (0, 0): [(0, -2), (1, -1)],
        (0, 1): [(1, -1)],
        (1, 0): [(2, -1)],
        (1, 1): [(2, -1)],
    }
    for n, (I, J) in enumerate(D1_CORNER):
        cube = acc[n]
        for k, m in terms[I, J]:
            cube = cube + nt(s3[k], xs(J, m, m))
        near = d1_store(d1, I, J)

        def store(a, b, v, I=I, J=J, near=near):
            near(a, b, v)
            r, c = 3 - (2 * I + a), 3 - (2 * J + b)
            swap[c // 2, pl.ds(r * B, B), pl.ds((c % 2) * B, B)] = v

        put_step(store, xs(I, J, J), cube, I, J, mask)

    known = {hc: s4[n] for n, hc in enumerate(D1_CORNER)}
    known.update({hc: s3[n] for n, hc in enumerate(S_CROSS)})
    for I, J in S_CROSS:
        lo, hi = I - 2, J + 2
        cube = sum(nt(known[I, m], xs(J, m, m)) for m in range(lo, hi + 1))
        put_step(d1_store(d1, I, J), xs(I, J, J), cube, I, J, mask)


def corner(pa, xb01, xt, s4, acc, mk, d1):
    return pl.pallas_call(
        corner_kernel,
        out_shape=[
            jax.ShapeDtypeStruct((3, T, T), BF),
            jax.ShapeDtypeStruct((7, 5 * T, T), BF),
            jax.ShapeDtypeStruct((2, 2 * T, T), BF),
        ],
        in_specs=[VM] * 7,
        out_specs=[VM] * 3,
        scratch_shapes=[pltpu.VMEM((4, T, 5 * T), BF)],
        input_output_aliases={6: 1},
        compiler_params=pltpu.CompilerParams(vmem_limit_bytes=24 * MIB),
        cost_estimate=pl.CostEstimate(flops=2 * 30 * T * T * T, bytes_accessed=4 * MIB, transcendentals=0),
        name="corner",
    )(pa, xb01, xt, s4, acc, mk, d1)


D1_HALO = [(-2, 0), (-1, 0), (-1, 1), (-1, -1), (-1, -2), (-2, -1), (-2, -2)]
H = R // 2
Q = 2 * SHARE


def finish_kernel(pa, pb, xb01, xt, s4, s3, mk, swapped, d1_in, d1, keep, send, xh, sb, left, s1):
    del d1_in
    layer = lax.axis_index("layer")
    flip = lax.rem(layer, 2)
    chip_rows = pl.multiple_of(lax.div(layer, 2) * Q, Q)
    mask = halo_mask(mk, pa)
    one = eye()
    unpack(pa, pb, xh, one)
    put_cross(xh, xt)
    xs = rows_of(xb01, xh)

    def spos(I, J):
        return (I + 2, slice(None), pl.ds((J - I + 2) * T, T))

    def ss(I, lo, hi):
        return sb[I + 2, :, pl.ds((lo - I + 2) * T, (hi - lo + 1) * T)]

    for n, (I, J) in enumerate(D1_CORNER):
        sb[spos(I, J)] = s4[n]
    for n, (I, J) in enumerate(S_CROSS):
        sb[spos(I, J)] = s3[n]
        sb[spos(J, I)] = nt(one, s3[n]).astype(BF)
    for I, J in [(-1, -1), (-2, -2), (-1, -2), (-1, -3), (-2, -3), (-2, -4)]:
        lo, hi = I - 2, J + 2

        def store(a, b, v, I=I, J=J):
            sb[I + 2, pl.ds(a * B, B), pl.ds((J - I + 2) * T + b * B, B)] = v

        put_masked(store, nt(xs(I, lo, hi), xs(J, lo, hi)), I, J, mask)
    sb[spos(-2, -1)] = nt(one, ss(-1, -2, -2)).astype(BF)

    for I, J in D1_HALO:
        lo, hi = max(I, J) - 2, min(I, J) + 2
        put_step(d1_store(d1, I, J), xs(I, J, J), nt(ss(I, lo, hi), xs(J, lo, hi)), I, J, mask)

    for i in range(H):
        I, a = i // 2, i % 2
        for J in range(-2, 5):
            dst = (pl.ds(i * Q, Q), pl.ds((J + 2) * T, T))
            if abs(I - J) <= 2:
                left[dst] = d1[J + 2, pl.ds((I - J + 2) * T + a * B + chip_rows, Q), :]
            else:
                left[dst] = jnp.zeros((Q, T), BF)

    def product(lhs, J):
        i0, i1 = max(0, 2 * J - 4), min(H - 1, 2 * J + 5)
        k0, k1 = max(J - 2, -2), min(J + 2, 4)
        rows = pl.ds(i0 * Q, (i1 - i0 + 1) * Q)
        if J < 3:
            a = lhs[rows, pl.ds((k0 + 2) * T, (k1 - k0 + 1) * T)]
            return i0, i1, nn(a, d1[J + 2, pl.ds((k0 - J + 2) * T, (k1 - k0 + 1) * T), :])
        a, b = lhs[rows, pl.ds((k0 + 2) * T, (3 - k0) * T)], lhs[rows, pl.ds(5 * T, 2 * T)]
        return i0, i1, nn(a, d1[J + 2, pl.ds((k0 - J + 2) * T, (3 - k0) * T), :]) + nn(b, swapped[J - 3])

    for J in range(4, -3, -1):
        i0, i1, s = product(left, J)
        for i in range(H):
            for b in range(2):
                j = 2 * J + b
                dst = (pl.ds(i * Q, Q), pl.ds((J + 2) * T + b * B, B))
                if abs(i - j) <= 4 and i0 <= i <= i1:
                    q = s[(i - i0) * Q : (i - i0 + 1) * Q, b * B : (b + 1) * B]
                    s1[dst] = (q * mask(i, j)).astype(BF)
                else:
                    s1[dst] = jnp.zeros((Q, B), BF)

    for J in range(4, -3, -1):
        i0, i1, cube = product(s1, J)
        for i in range(i0, i1 + 1):
            for b in range(2):
                j = 2 * J + b
                if abs(i - j) > 4:
                    continue
                q = cube[(i - i0) * Q : (i - i0 + 1) * Q, b * B : (b + 1) * B] * mask(i, j)
                x = left[pl.ds(i * Q, Q), pl.ds((J + 2) * T + b * B, B)].astype(F32)
                v = (3.0 * x - q * SCALE) * 0.5
                w = j - i + 4
                near = jnp.where(flip == 1, H - 1 - i, i)
                slot = jnp.where(flip == 1, W - 1 - w, w)
                lo, hi = v[:SHARE].astype(BF), v[SHARE:].astype(BF)
                keep[near, slot] = jnp.where(flip == 1, hi, lo)
                send[near, slot] = jnp.where(flip == 1, lo, hi)


def finish(pa, pb, xb01, xt, s4, s3, mk, swapped, d1):
    return pl.pallas_call(
        finish_kernel,
        out_shape=[
            jax.ShapeDtypeStruct((7, 5 * T, T), BF),
            jax.ShapeDtypeStruct((H, W, SHARE, B), BF),
            jax.ShapeDtypeStruct((H, W, SHARE, B), BF),
        ],
        in_specs=[VM] * 9,
        out_specs=[VM] * 3,
        scratch_shapes=[
            pltpu.VMEM((4, T, 5 * T), BF),
            pltpu.VMEM((4, T, 5 * T), BF),
            pltpu.VMEM((H * Q, 7 * T), BF),
            pltpu.VMEM((H * Q, 7 * T), BF),
        ],
        input_output_aliases={8: 0},
        compiler_params=pltpu.CompilerParams(vmem_limit_bytes=36 * MIB),
        cost_estimate=pl.CostEstimate(flops=2 * 120 * T * T * T, bytes_accessed=8 * MIB, transcendentals=0),
        name="finish",
    )(pa, pb, xb01, xt, s4, s3, mk, swapped, d1)


def join_kernel(keep, other, out, sem):
    flip = flip_core()
    a = pltpu.make_async_copy(keep, out.at[pl.ds(jnp.where(flip == 1, H, 0), H)], sem.at[0])
    b = pltpu.make_async_copy(other, out.at[pl.ds(jnp.where(flip == 1, 0, H), H)], sem.at[1])
    a.start()
    b.start()
    a.wait()
    b.wait()


def join(keep, other):
    return pl.pallas_call(
        join_kernel,
        out_shape=jax.ShapeDtypeStruct((R, W, SHARE, B), BF),
        in_specs=[VM, VM],
        out_specs=HBM,
        scratch_shapes=[pltpu.SemaphoreType.DMA((2,))],
        compiler_params=pltpu.CompilerParams(vmem_limit_bytes=2 * MIB),
        name="join",
    )(keep, other)


def chain(layers, grid):
    pairs = []
    for l in range(layers):
        for g in range(grid):
            pairs.append((l * grid + g, l * grid + (g + 1 if l % 2 == 0 else g - 1) % grid))
    return pairs


def per_device(x, ret):
    layers, grid = lax.axis_size("layer"), lax.axis_size("grid")
    cores = [(l, l ^ 1) for l in range(layers)]
    pairs = chain(layers, grid)
    x = pltpu.with_memory_space_constraint(x, pltpu.HBM)
    ret = pltpu.with_memory_space_constraint(ret, pltpu.HBM)
    pa = pack(x, ret, A_OFF, A_PACK, MASKS, A_ROWS, "pack_corner")
    pa = lax.ppermute(pa, ("layer", "grid"), pairs)
    pb = pack(x, ret, B_OFF + C_OFF, C_PACK, [], B_ROWS, "pack_deep")
    pb = lax.ppermute(pb, ("layer", "grid"), pairs)
    xb01, xt, s4, acc, d1, mk = early(x, ret)
    s3, d1, swap = corner(pa, xb01, xt, s4, acc, mk, d1)
    swapped = lax.ppermute(swap, "layer", cores)
    _, keep, send = finish(pa, pb, xb01, xt, s4, s3, mk, swapped, d1)
    other = lax.ppermute(send, "layer", cores)
    return join(keep, other)


def solution(mesh):
    return jax.shard_map(
        per_device,
        mesh=mesh,
        in_specs=(P("grid", None, None, None), P("grid", None)),
        out_specs=P("grid", None, "layer", None),
        check_vma=False,
    )
```

```python
import jax
import jax.numpy as jnp
from jax import lax
from jax.experimental import pallas as pl
from jax.experimental.pallas import tpu as pltpu
from jax.sharding import PartitionSpec as P

B = 128
T = 256
R = 10
W = 9
SHARE = 32
SCALE = 1.0 / (4.0 * W * B)
BF = jnp.bfloat16
F32 = jnp.float32
MIB = 2**20

A_OFF = [(5, 4), (6, 4), (7, 4), (6, 5), (7, 5), (7, 6)]
A_PACK = [(4, 5), (6, 7)]
A_PAIRS = [(h, c) for h in range(4, 8) for c in range(4, h + 1)]
B_OFF = [(h, c) for h in range(4, 8) for c in range(h - 4, 4)]
C_OFF = [(h - 4, c - 4) for h, c in A_OFF]
C_PACK = [(h - 4, c - 4) for h, c in A_PACK]
MASKS = A_PAIRS + B_OFF
NA = len(A_OFF) + 2
NB = len(B_OFF) + len(C_OFF) + 2
A_ROWS = NA * B + 32
B_ROWS = NB * B + 16

HBM = pl.BlockSpec(memory_space=pltpu.HBM)
VM = pl.BlockSpec(memory_space=pltpu.VMEM)


def nt(a, b):
    return lax.dot_general(a, b, (((1,), (1,)), ((), ())), preferred_element_type=F32)


def nn(a, b):
    return lax.dot_general(a, b, (((1,), (0,)), ((), ())), preferred_element_type=F32)


def flip_core():
    return lax.rem(lax.axis_index("layer"), 2)


def place(flip, i, w):
    return jnp.where(flip == 1, R - 1 - i, i), jnp.where(flip == 1, W - 1 - w, w)


def own_slot(i, j):
    if not 0 <= i < R:
        i, j = j, i
    return i, j - i + 4


def smem_mask(ret, flip, i, j):
    row, slot = place(flip, *own_slot(i, j))
    return (ret[row, slot] != 0).astype(F32)


def iotas(n):
    return lax.broadcasted_iota(jnp.int32, (n, n), 0), lax.broadcasted_iota(jnp.int32, (n, n), 1)


def eye():
    r, c = iotas(T)
    return (r == c).astype(F32).astype(BF)


def whole(row16):
    return jnp.concatenate([row16] * (B // 16), axis=0)


def put_masked(store, tile, I, J, mask):
    for a in range(2):
        for b in range(2):
            i, j = 2 * I + a, 2 * J + b
            if abs(i - j) > 4:
                store(a, b, jnp.zeros((B, B), BF))
            else:
                store(a, b, (tile[a * B : (a + 1) * B, b * B : (b + 1) * B] * mask(i, j)).astype(BF))


def put_step(store, x, cube, I, J, mask):
    for a in range(2):
        for b in range(2):
            i, j = 2 * I + a, 2 * J + b
            if abs(i - j) > 4:
                store(a, b, jnp.zeros((B, B), BF))
            else:
                q = cube[a * B : (a + 1) * B, b * B : (b + 1) * B] * mask(i, j)
                xq = x[a * B : (a + 1) * B, b * B : (b + 1) * B].astype(F32)
                store(a, b, ((3.0 * xq - q * SCALE) * 0.5).astype(BF))


def at(ref, *lead):
    def store(a, b, v):
        ref[(*lead, pl.ds(a * B, B), pl.ds(b * B, B))] = v

    return store


def d1_store(d1, I, J):
    def store(a, b, v):
        d1[J + 2, pl.ds((I - J + 2) * T + a * B, B), pl.ds(b * B, B)] = v

    return store


def send_rows(out, off, packs, masks, get, mask_of):
    r, c = iotas(B)
    aux = (len(off) + len(packs)) * B
    for n, (h, g) in enumerate(off):
        out[pl.ds(n * B, B), :] = get(h, g)
    rows = [mask_of(h, g) for h, g in masks]
    for k, (h, g) in enumerate(packs):
        first, second = get(h, h).astype(F32), get(g, g).astype(F32)
        out[pl.ds((len(off) + k) * B, B), :] = jnp.where(r <= c, first, second).astype(BF)
        rows.append(jnp.sum(jnp.where(r == c, second, 0.0), axis=0, keepdims=True))
    n_rows = out.shape[0] - aux
    rows.append(jnp.zeros((n_rows - len(rows), B), F32))
    out[pl.ds(aux, n_rows), :] = jnp.concatenate(rows, axis=0).astype(BF)


def pack_corner_kernel(x, ret, out, buf, smem, sem, ret_sem):
    flip = flip_core()
    load = pltpu.make_async_copy(ret, smem, ret_sem)
    load.start()
    blocks = A_OFF + [(h, h) for pair in A_PACK for h in pair]
    copies = {}
    for n, (h, g) in enumerate(blocks):
        row, slot = place(flip, h + 2, g - h + 4)
        copies[h, g] = (pltpu.make_async_copy(x.at[row, slot], buf.at[n], sem.at[n]), n)
        copies[h, g][0].start()
    load.wait()

    def get(h, g):
        copy, n = copies[h, g]
        copy.wait()
        m = jnp.full((16, B), smem_mask(smem, flip, h + 2, g + 2), F32).astype(BF)
        return buf[n] * whole(m)

    def mask_of(h, g):
        return jnp.full((1, B), smem_mask(smem, flip, h + 2, g + 2), F32)

    send_rows(out, A_OFF, A_PACK, MASKS, get, mask_of)


def pack_corner(x, ret):
    n = len(A_OFF) + 2 * len(A_PACK)
    return pl.pallas_call(
        pack_corner_kernel,
        out_shape=jax.ShapeDtypeStruct((A_ROWS, B), BF),
        in_specs=[HBM, HBM],
        out_specs=VM,
        scratch_shapes=[
            pltpu.VMEM((n, B, B), BF),
            pltpu.SMEM((R, W), jnp.int32),
            pltpu.SemaphoreType.DMA((n,)),
            pltpu.SemaphoreType.DMA,
        ],
        compiler_params=pltpu.CompilerParams(vmem_limit_bytes=4 * MIB),
        cost_estimate=pl.CostEstimate(flops=1000, bytes_accessed=MIB, transcendentals=0),
        name="pack_corner",
    )(x, ret)


MK = R * W + 6


def pack_deep_kernel(x, ret, first, out, xin, mk, smem, sem, ret_sem):
    del first
    flip = flip_core()
    load = pltpu.make_async_copy(ret, smem, ret_sem)
    load.start()
    copies = {}
    for i in [*range(2, R), 0, 1]:
        row, _ = place(flip, i, 0)
        copies[i] = pltpu.make_async_copy(x.at[row], xin.at[i], sem.at[i])
        copies[i].start()
    load.wait()
    for i in range(R):
        for w in range(W):
            mk[pl.ds(i * W + w, 1), :] = jnp.full((1, B), smem_mask(smem, flip, i, i + w - 4), F32)
    mk[pl.ds(R * W, MK - R * W), :] = jnp.zeros((MK - R * W, B), F32)
    for i in range(2, R):
        copies[i].wait()

    def get(h, g):
        _, slot = place(flip, h + 2, g - h + 4)
        m = jnp.full((16, B), smem_mask(smem, flip, h + 2, g + 2), F32).astype(BF)
        return xin[h + 2, slot] * whole(m)

    send_rows(out, B_OFF + C_OFF, C_PACK, [], get, None)
    copies[0].wait()
    copies[1].wait()


def pack_deep(x, ret, first):
    return pl.pallas_call(
        pack_deep_kernel,
        out_shape=[
            jax.ShapeDtypeStruct((B_ROWS, B), BF),
            jax.ShapeDtypeStruct((R, W, B, B), BF),
            jax.ShapeDtypeStruct((MK, B), F32),
        ],
        in_specs=[HBM, HBM, VM],
        out_specs=[VM] * 3,
        scratch_shapes=[
            pltpu.SMEM((R, W), jnp.int32),
            pltpu.SemaphoreType.DMA((R,)),
            pltpu.SemaphoreType.DMA,
        ],
        compiler_params=pltpu.CompilerParams(vmem_limit_bytes=8 * MIB),
        cost_estimate=pl.CostEstimate(flops=1000, bytes_accessed=4 * MIB, transcendentals=0),
        name="pack_deep",
    )(x, ret, first)


D1_EARLY = [(0, 2), (2, 0), (1, 2), (2, 1), (2, 2), (1, 3)]
D1_CORNER = [(0, 0), (0, 1), (1, 0), (1, 1)]
S_EARLY = [(0, 0), (0, 1), (0, 2), (1, 1), (1, 2), (1, 3), (2, 2), (2, 3), (2, 4)]
S_TURNED = [(0, 1), (0, 2), (1, 2)]
D1 = jax.ShapeDtypeStruct((7, 5 * T, T), BF)
HROWS = jax.ShapeDtypeStruct((4, T, 5 * T), BF)


def xh_at(I, J):
    return (I + 4, slice(None), pl.ds((J - I + 2) * T, T))


def sb_at(I, J):
    return (I + 2, slice(None), pl.ds((J - I + 2) * T, T))


def sb_store(sb, I, J):
    def store(a, b, v):
        sb[I + 2, pl.ds(a * B, B), pl.ds((J - I + 2) * T + b * B, B)] = v

    return store


def rows_of(xb01, xh):
    def xs(I, lo, hi):
        cols = pl.ds((lo - I + 2) * T, (hi - lo + 1) * T)
        return xb01[I, :, cols] if I >= 0 else xh[I + 4, :, cols]

    return xs


def square_rows(sb):
    def ss(I, lo, hi):
        return sb[I + 2, :, pl.ds((lo - I + 2) * T, (hi - lo + 1) * T)]

    return ss


def own_masks(mk):
    def mask(i, j):
        i, w = own_slot(i, j)
        return mk[pl.ds(i * W + w, 1), :]

    return mask


def early_kernel(xin, mk, xb01, xh, sb, acc, d1, centre, xb, s):
    flip = flip_core()
    mask = own_masks(mk)

    for I in range(5):
        xb[I, pl.ds(0, B), pl.ds(9 * B, B)] = jnp.zeros((B, B), BF)
        xb[I, pl.ds(B, B), pl.ds(0, B)] = jnp.zeros((B, B), BF)
        for a in range(2):
            i = 2 * I + a
            for w in range(W):
                _, slot = place(flip, i, w)
                m = jnp.broadcast_to(mask(i, i + w - 4), (16, B)).astype(BF)
                v = xin[i, slot] * whole(m)
                xb[I, pl.ds(a * B, B), pl.ds((a + w) * B, B)] = v
                if I < 2:
                    xb01[I, pl.ds(a * B, B), pl.ds((a + w) * B, B)] = v
        if I < 2:
            xb01[I, pl.ds(0, B), pl.ds(9 * B, B)] = jnp.zeros((B, B), BF)
            xb01[I, pl.ds(B, B), pl.ds(0, B)] = jnp.zeros((B, B), BF)

    def xs(I, lo, hi):
        return xb[I, :, pl.ds((lo - I + 2) * T, (hi - lo + 1) * T)]

    def ss(I, lo, hi):
        return s[I, :, pl.ds((lo - I + 2) * T, (hi - lo + 1) * T)]

    one = eye()
    for I, K in S_CROSS:
        xh[xh_at(K, I)] = nt(one, xs(I, K, K)).astype(BF)

    for I, J in S_EARLY:
        def store(a, b, v, I=I, J=J):
            s[I, pl.ds(a * B, B), pl.ds((J - I + 2) * T + b * B, B)] = v

        put_masked(store, nt(xs(I, J - 2, I + 2), xs(J, J - 2, I + 2)), I, J, mask)
        if (I, J) in S_TURNED:
            s[J, :, pl.ds((I - J + 2) * T, T)] = nt(one, ss(I, J, J)).astype(BF)

    for n, (I, J) in enumerate(D1_CORNER):
        sb[sb_at(I, J)] = ss(I, J, J)
        lo, hi = max(0, I - 2, J - 2), min(I, J) + 2
        acc[n] = nt(ss(I, lo, hi), xs(J, lo, hi))

    for I, J in D1_EARLY:
        lo, hi = max(I, J) - 2, min(I, J) + 2
        store = put_swap(d1_store(d1, I, J), centre, CENTRE, I, J)
        put_step(store, xs(I, J, J), nt(ss(I, lo, hi), xs(J, lo, hi)), I, J, mask)


def early(xin, mk):
    return pl.pallas_call(
        early_kernel,
        out_shape=[
            jax.ShapeDtypeStruct((2, T, 5 * T), BF),
            HROWS,
            HROWS,
            jax.ShapeDtypeStruct((4, T, T), F32),
            D1,
            jax.ShapeDtypeStruct((len(CENTRE), B, B), BF),
        ],
        in_specs=[VM] * 2,
        out_specs=[VM] * 6,
        scratch_shapes=[pltpu.VMEM((5, T, 5 * T), BF), pltpu.VMEM((3, T, 5 * T), BF)],
        compiler_params=pltpu.CompilerParams(vmem_limit_bytes=24 * MIB),
        cost_estimate=pl.CostEstimate(flops=2 * T * T * T, bytes_accessed=1000, transcendentals=0),
        name="early",
    )(xin, mk)


def halo_mask(mk, pa):
    own = own_masks(mk)

    def mask(i, j):
        if 0 <= i < R or 0 <= j < R:
            return own(i, j)
        n = MASKS.index((max(i, j) + 8, min(i, j) + 8))
        return pa[pl.ds(NA * B + n, 1), :].astype(F32)

    return mask


def unpack(ref, off, packs, base, aux, xh, one):
    r, c_ = iotas(B)
    n_off = len(off)

    def dst(h, c):
        I, J = h // 2 - 4, c // 2 - 4
        return (I + 4, pl.ds((h % 2) * B, B), pl.ds((J - I + 2) * T + (c % 2) * B, B))

    tiles = set()
    for n, (h, c) in enumerate(off):
        xh[dst(h, c)] = ref[pl.ds(n * B, B), :]
        if h // 2 == c // 2:
            xh[dst(c, h)] = nt(one[:B, :B], ref[pl.ds(n * B, B), :]).astype(BF)
        else:
            tiles.add((h // 2 - 4, c // 2 - 4))
    for k, (h, g) in enumerate(packs):
        both = ref[pl.ds((base + k) * B, B), :]
        turned = nt(one[:B, :B], both)
        both = both.astype(F32)
        xh[dst(h, h)] = jnp.where(r <= c_, both, turned).astype(BF)
        other = jnp.where(r < c_, turned, both)
        diagonal = ref[pl.ds(aux + k, 1), :].astype(F32)
        xh[dst(g, g)] = jnp.where(r == c_, diagonal, other).astype(BF)
    for I, J in sorted(tiles):
        for a in range(2):
            for b in range(2):
                if abs(2 * I + a - 2 * J - b) > 4:
                    xh[dst(2 * I + a + 8, 2 * J + b + 8)] = jnp.zeros((B, B), BF)
        xh[xh_at(J, I)] = nt(one, xh[xh_at(I, J)]).astype(BF)


S_CROSS = [(0, -2), (0, -1), (1, -1)]
CENTRE = [(r, c) for r in range(4, 9) for c in range(2, 9) if abs(r - c) <= 4 and not (r < 6 and c < 6) and (r < 6 or c < 6)]
CORNER = [(r, c) for r in range(6, 9) for c in range(6, 9)]


def put_swap(store, swap, blocks, I, J):
    def both(a, b, v):
        store(a, b, v)
        at = (R - 1 - 2 * I - a, R - 1 - 2 * J - b)
        if at in blocks:
            swap[blocks.index(at)] = v

    return both


def corner_kernel(pa, xb01, acc, mk, xh_in, sb_in, d1_in, xh, sb, d1, swap):
    del xh_in, sb_in, d1_in
    mask = halo_mask(mk, pa)
    one = eye()
    unpack(pa, A_OFF, A_PACK, len(A_OFF), NA * B + len(MASKS), xh, one)
    xs = rows_of(xb01, xh)
    ss = square_rows(sb)

    for I, J in S_CROSS:
        put_masked(sb_store(sb, I, J), nt(xs(I, I - 2, J + 2), xs(J, I - 2, J + 2)), I, J, mask)
    terms = {(0, 0): -2, (0, 1): -1, (1, 0): -1, (1, 1): -1}
    for n, (I, J) in enumerate(D1_CORNER):
        lo = terms[I, J]
        cube = acc[n] + nt(ss(I, lo, -1), xs(J, lo, -1))
        store = put_swap(d1_store(d1, I, J), swap, CORNER, I, J)
        put_step(store, xs(I, J, J), cube, I, J, mask)
    for I, J in S_CROSS:
        cube = nt(ss(I, I - 2, J + 2), xs(J, I - 2, J + 2))
        put_step(d1_store(d1, I, J), xs(I, J, J), cube, I, J, mask)


def corner(pa, xb01, acc, mk, xh, sb, d1):
    return pl.pallas_call(
        corner_kernel,
        out_shape=[HROWS, HROWS, D1, jax.ShapeDtypeStruct((len(CORNER), B, B), BF)],
        in_specs=[VM] * 7,
        out_specs=[VM] * 4,
        input_output_aliases={4: 0, 5: 1, 6: 2},
        compiler_params=pltpu.CompilerParams(vmem_limit_bytes=16 * MIB),
        cost_estimate=pl.CostEstimate(flops=2 * 32 * T * T * T, bytes_accessed=1000, transcendentals=0),
        name="corner",
    )(pa, xb01, acc, mk, xh, sb, d1)


H = R // 2
Q = 2 * SHARE
M = H * Q
S_PART = [(-1, -1), (-2, -2), (-1, -2)]
D1_HALO = [(-2, 0), (-1, 0), (-1, 1), (-1, -1), (-1, -2), (-2, -1), (-2, -2)]
LEFT = jax.ShapeDtypeStruct((M, 7 * T), BF)


def chip_share():
    layer = lax.axis_index("layer")
    return lax.rem(layer, 2), pl.multiple_of(lax.div(layer, 2) * Q, Q)


def in_rows(J):
    return max(0, 2 * J - 4), min(H - 1, 2 * J + 5)


def put_left(left, d1, i, J, chip_rows):
    I, a = i // 2, i % 2
    dst = (pl.ds(i * Q, Q), pl.ds((J + 2) * T, T))
    if abs(I - J) <= 2:
        left[dst] = d1[J + 2, pl.ds((I - J + 2) * T + a * B + chip_rows, Q), :]
    else:
        left[dst] = jnp.zeros((Q, T), BF)


def product(lhs, d1, J, i0, i1, k0, k1):
    a = lhs[pl.ds(i0 * Q, (i1 - i0 + 1) * Q), pl.ds((k0 + 2) * T, (k1 - k0 + 1) * T)]
    return nn(a, d1[J + 2, pl.ds((k0 - J + 2) * T, (k1 - k0 + 1) * T), :])


def beside_kernel(xb01, mk, xh, sb, d1_in, d1, left, sp, xp, s1p):
    del mk, d1_in
    _, chip_rows = chip_share()
    one = eye()
    xs = rows_of(xb01, xh)

    def ss(I, m):
        return nt(one, sb[sb_at(m, I)]).astype(BF)

    turned = {(-2, 0): ss(-2, 0), (-1, 0): ss(-1, 0), (-1, 1): ss(-1, 1)}
    for n, (I, J) in enumerate(S_PART):
        sp[n] = nt(xs(I, -2, J + 2 if I >= J else I + 2), xs(J, -2, J + 2 if I >= J else I + 2))
    for n, (I, J) in enumerate(D1_HALO):
        total = None
        for m in range(min(I, J) + 3):
            term = nt(turned[I, m], xs(J, m, m))
            total = term if total is None else total + term
        xp[n] = total
    for i in range(H):
        for J in range(-2, 5):
            if not (i == 4 and J >= 3):
                put_left(left, d1, i, J, chip_rows)
    for J, k1 in [(-2, 0), (-1, 1), (0, 2)]:
        i0, i1 = in_rows(J)
        s1p[pl.ds(i0 * Q, (i1 - i0 + 1) * Q), pl.ds((J + 2) * T, T)] = product(left, d1, J, i0, i1, 0, k1)


def beside(xb01, mk, xh, sb, d1):
    return pl.pallas_call(
        beside_kernel,
        out_shape=[
            D1,
            LEFT,
            jax.ShapeDtypeStruct((len(S_PART), T, T), F32),
            jax.ShapeDtypeStruct((len(D1_HALO), T, T), F32),
            jax.ShapeDtypeStruct((M, 3 * T), F32),
        ],
        in_specs=[VM] * 5,
        out_specs=[VM] * 5,
        input_output_aliases={4: 0},
        compiler_params=pltpu.CompilerParams(vmem_limit_bytes=16 * MIB),
        cost_estimate=pl.CostEstimate(flops=1000, bytes_accessed=1000, transcendentals=0),
        name="beside",
    )(xb01, mk, xh, sb, d1)


def put_square(s1, s, J, i0, mask):
    i1 = i0 + s.shape[0] // Q - 1
    for i in range(H):
        for b in range(2):
            j = 2 * J + b
            dst = (pl.ds(i * Q, Q), pl.ds((J + 2) * T + b * B, B))
            if abs(i - j) <= 4:
                assert i0 <= i <= i1
                q = s[(i - i0) * Q : (i - i0 + 1) * Q, b * B : (b + 1) * B]
                s1[dst] = (q * mask(i, j)).astype(BF)
            else:
                s1[dst] = jnp.zeros((Q, B), BF)


def swapped_kernel(centre, swapped, mk, left_in, d1_in, left, d1, s1, s1q, x2p):
    del left_in, d1_in
    _, chip_rows = chip_share()
    mask = own_masks(mk)

    def put(r, c, v):
        d1_store(d1, r // 2, c // 2)(r % 2, c % 2, v)

    for ref, blocks in ((centre, CENTRE), (swapped, CORNER)):
        for n, (r, c) in enumerate(blocks):
            put(r, c, ref[n])
    for k in range(4, R):
        put(k, R - 1, jnp.zeros((B, B), BF))
        if k < R - 1:
            put(R - 1, k, jnp.zeros((B, B), BF))
    put(7, 2, jnp.zeros((B, B), BF))
    for J in (3, 4):
        put_left(left, d1, 4, J, chip_rows)
    for J in (2, 3, 4):
        i0, i1 = in_rows(J)
        put_square(s1, product(left, d1, J, i0, i1, max(J - 2, 0), 4), J, i0, mask)
    s1q[...] = product(left, d1, 1, 0, H - 1, 0, 3)
    for J in range(5):
        i0, i1 = in_rows(J)
        part = product(s1, d1, J, i0, i1, 2, min(J + 2, 4))
        x2p[pl.ds(i0 * Q, (i1 - i0 + 1) * Q), pl.ds(J * T, T)] = part


def use_swapped(centre, swapped, mk, left, d1):
    return pl.pallas_call(
        swapped_kernel,
        out_shape=[
            LEFT,
            D1,
            LEFT,
            jax.ShapeDtypeStruct((M, T), F32),
            jax.ShapeDtypeStruct((M, 5 * T), F32),
        ],
        in_specs=[VM] * 5,
        out_specs=[VM] * 5,
        input_output_aliases={3: 0, 4: 1},
        compiler_params=pltpu.CompilerParams(vmem_limit_bytes=16 * MIB),
        cost_estimate=pl.CostEstimate(flops=1000, bytes_accessed=1000, transcendentals=0),
        name="use_swapped",
    )(centre, swapped, mk, left, d1)


def finish_kernel(pa, pb, xb01, mk, left, sp, xp, s1p, s1q, x2p, xh_in, sb_in, d1_in, s1_in, xh, sb, d1, s1, keep, send):
    del xh_in, sb_in, d1_in, s1_in
    flip, _ = chip_share()
    mask = halo_mask(mk, pa)
    one = eye()
    unpack(pb, B_OFF + C_OFF, C_PACK, NB - 2, NB * B, xh, one)
    xs = rows_of(xb01, xh)
    ss = square_rows(sb)

    for n, (I, J) in enumerate(S_PART):
        lo = max(I, J) - 2
        put_masked(sb_store(sb, I, J), sp[n] + nt(xs(I, lo, -3), xs(J, lo, -3)), I, J, mask)
    sb[sb_at(-2, -1)] = nt(one, ss(-1, -2, -2)).astype(BF)
    for I, J in [(-1, -3), (-2, -3), (-2, -4)]:
        put_masked(sb_store(sb, I, J), nt(xs(I, I - 2, J + 2), xs(J, I - 2, J + 2)), I, J, mask)

    for n, (I, J) in enumerate(D1_HALO):
        lo = max(I, J) - 2
        put_step(d1_store(d1, I, J), xs(I, J, J), xp[n] + nt(ss(I, lo, -1), xs(J, lo, -1)), I, J, mask)

    for J in (1, 0, -1, -2):
        i0, i1 = in_rows(J)
        near = min(i1, 3)
        part = product(left, d1, J, i0, near, max(J - 2, -2), -1)
        rows = pl.ds(i0 * Q, (near - i0 + 1) * Q)
        rest = s1q if J == 1 else s1p
        cols = pl.ds(0, T) if J == 1 else pl.ds((J + 2) * T, T)
        total = part + rest[rows, cols]
        if i1 > near:
            total = jnp.concatenate([total, rest[pl.ds((near + 1) * Q, (i1 - near) * Q), cols]], axis=0)
        put_square(s1, total, J, i0, mask)

    for J in range(4, -3, -1):
        i0, i1 = in_rows(J)
        rows = pl.ds(i0 * Q, (i1 - i0 + 1) * Q)
        k0 = max(J - 2, -2)
        if J == 4:
            cube = x2p[rows, pl.ds(J * T, T)]
        else:
            cube = product(s1, d1, J, i0, i1, k0, min(J + 2, 1))
            if J >= 0:
                cube = cube + x2p[rows, pl.ds(J * T, T)]
        for i in range(i0, i1 + 1):
            for b in range(2):
                j = 2 * J + b
                if abs(i - j) > 4:
                    continue
                q = cube[(i - i0) * Q : (i - i0 + 1) * Q, b * B : (b + 1) * B] * mask(i, j)
                x = left[pl.ds(i * Q, Q), pl.ds((J + 2) * T + b * B, B)].astype(F32)
                v = (3.0 * x - q * SCALE) * 0.5
                w = j - i + 4
                near = jnp.where(flip == 1, H - 1 - i, i)
                slot = jnp.where(flip == 1, W - 1 - w, w)
                lo, hi = v[:SHARE].astype(BF), v[SHARE:].astype(BF)
                keep[near, slot] = jnp.where(flip == 1, hi, lo)
                send[near, slot] = jnp.where(flip == 1, lo, hi)


def finish(pa, pb, xb01, mk, left, sp, xp, s1p, s1q, x2p, xh, sb, d1, s1):
    half = jax.ShapeDtypeStruct((H, W, SHARE, B), BF)
    return pl.pallas_call(
        finish_kernel,
        out_shape=[HROWS, HROWS, D1, LEFT, half, half],
        in_specs=[VM] * 14,
        out_specs=[VM] * 6,
        input_output_aliases={10: 0, 11: 1, 12: 2, 13: 3},
        compiler_params=pltpu.CompilerParams(vmem_limit_bytes=16 * MIB),
        cost_estimate=pl.CostEstimate(flops=2 * 70 * T * T * T, bytes_accessed=8 * MIB, transcendentals=0),
        name="finish",
    )(pa, pb, xb01, mk, left, sp, xp, s1p, s1q, x2p, xh, sb, d1, s1)


def join_kernel(keep, other, out, sem):
    flip = flip_core()
    a = pltpu.make_async_copy(keep, out.at[pl.ds(jnp.where(flip == 1, H, 0), H)], sem.at[0])
    b = pltpu.make_async_copy(other, out.at[pl.ds(jnp.where(flip == 1, 0, H), H)], sem.at[1])
    a.start()
    b.start()
    a.wait()
    b.wait()


def join(keep, other):
    return pl.pallas_call(
        join_kernel,
        out_shape=jax.ShapeDtypeStruct((R, W, SHARE, B), BF),
        in_specs=[VM, VM],
        out_specs=HBM,
        scratch_shapes=[pltpu.SemaphoreType.DMA((2,))],
        compiler_params=pltpu.CompilerParams(vmem_limit_bytes=2 * MIB),
        name="join",
    )(keep, other)


def chain(layers, grid):
    pairs = []
    for l in range(layers):
        for g in range(grid):
            pairs.append((l * grid + g, l * grid + (g + 1 if l % 2 == 0 else g - 1) % grid))
    return pairs


def per_device(x, ret):
    layers, grid = lax.axis_size("layer"), lax.axis_size("grid")
    cores = [(l, l ^ 1) for l in range(layers)]
    pairs = chain(layers, grid)
    x = pltpu.with_memory_space_constraint(x, pltpu.HBM)
    ret = pltpu.with_memory_space_constraint(ret, pltpu.HBM)
    pa = pack_corner(x, ret)
    pb, xin, mk = pack_deep(x, ret, pa)
    pa = lax.ppermute(pa, ("layer", "grid"), pairs)
    pb = lax.ppermute(pb, ("layer", "grid"), pairs)
    xb01, xh, sb, acc, d1, centre = early(xin, mk)
    centre = lax.ppermute(centre, "layer", cores)
    xh, sb, d1, swap = corner(pa, xb01, acc, mk, xh, sb, d1)
    swapped = lax.ppermute(swap, "layer", cores)
    d1, left, sp, xp, s1p = beside(xb01, mk, xh, sb, d1)
    left, d1, s1, s1q, x2p = use_swapped(centre, swapped, mk, left, d1)
    *_, keep, send = finish(pa, pb, xb01, mk, left, sp, xp, s1p, s1q, x2p, xh, sb, d1, s1)
    other = lax.ppermute(send, "layer", cores)
    return join(keep, other)


def solution(mesh):
    return jax.shard_map(
        per_device,
        mesh=mesh,
        in_specs=(P("grid", None, None, None), P("grid", None)),
        out_specs=P("grid", None, "layer", None),
        check_vma=False,
    )
```

```python
import jax
import jax.numpy as jnp
from jax import lax
from jax.experimental import pallas as pl
from jax.experimental.pallas import tpu as pltpu
from jax.sharding import PartitionSpec as P

B = 128
T = 256
R = 10
W = 9
SHARE = 32
SCALE = 1.0 / (4.0 * W * B)
BF = jnp.bfloat16
F32 = jnp.float32
MIB = 2**20

A_OFF = [(5, 4), (6, 4), (7, 4), (6, 5), (7, 5), (7, 6)]
A_PACK = [(4, 5), (6, 7)]
A_PAIRS = [(h, c) for h in range(4, 8) for c in range(4, h + 1)]
B_OFF = [(h, c) for h in range(4, 8) for c in range(h - 4, 4)]
C_OFF = [(h - 4, c - 4) for h, c in A_OFF]
C_PACK = [(h - 4, c - 4) for h, c in A_PACK]
MASKS = A_PAIRS + B_OFF
NA = len(A_OFF) + 2
NC = len(C_OFF) + 2
A_ROWS = NA * B + 32
B_ROWS = len(B_OFF) * B
C_ROWS = NC * B + 16

HBM = pl.BlockSpec(memory_space=pltpu.HBM)
VM = pl.BlockSpec(memory_space=pltpu.VMEM)


def nt(a, b):
    return lax.dot_general(a, b, (((1,), (1,)), ((), ())), preferred_element_type=F32)


def nn(a, b):
    return lax.dot_general(a, b, (((1,), (0,)), ((), ())), preferred_element_type=F32)


def flip_core():
    return lax.rem(lax.axis_index("layer"), 2)


def place(flip, i, w):
    return jnp.where(flip == 1, R - 1 - i, i), jnp.where(flip == 1, W - 1 - w, w)


def own_slot(i, j):
    if not 0 <= i < R:
        i, j = j, i
    return i, j - i + 4


def smem_mask(ret, flip, i, j):
    row, slot = place(flip, *own_slot(i, j))
    return (ret[row, slot] != 0).astype(F32)


def iotas(n):
    return lax.broadcasted_iota(jnp.int32, (n, n), 0), lax.broadcasted_iota(jnp.int32, (n, n), 1)


def eye():
    r, c = iotas(T)
    return (r == c).astype(F32).astype(BF)


def whole(row16):
    return jnp.concatenate([row16] * (B // 16), axis=0)


def put_masked(store, tile, I, J, mask):
    for a in range(2):
        for b in range(2):
            i, j = 2 * I + a, 2 * J + b
            if abs(i - j) > 4:
                store(a, b, jnp.zeros((B, B), BF))
            else:
                store(a, b, (tile[a * B : (a + 1) * B, b * B : (b + 1) * B] * mask(i, j)).astype(BF))


def put_step(store, x, cube, I, J, mask):
    for a in range(2):
        for b in range(2):
            i, j = 2 * I + a, 2 * J + b
            if abs(i - j) > 4:
                store(a, b, jnp.zeros((B, B), BF))
            else:
                q = cube[a * B : (a + 1) * B, b * B : (b + 1) * B] * mask(i, j)
                xq = x[a * B : (a + 1) * B, b * B : (b + 1) * B].astype(F32)
                store(a, b, ((3.0 * xq - q * SCALE) * 0.5).astype(BF))


def at(ref, *lead):
    def store(a, b, v):
        ref[(*lead, pl.ds(a * B, B), pl.ds(b * B, B))] = v

    return store


def d1_store(d1, I, J):
    def store(a, b, v):
        d1[J + 2, pl.ds((I - J + 2) * T + a * B, B), pl.ds(b * B, B)] = v

    return store


def send_rows(out, off, packs, masks, get, mask_of):
    r, c = iotas(B)
    aux = (len(off) + len(packs)) * B
    for n, (h, g) in enumerate(off):
        out[pl.ds(n * B, B), :] = get(h, g)
    rows = [mask_of(h, g) for h, g in masks]
    for k, (h, g) in enumerate(packs):
        first, second = get(h, h).astype(F32), get(g, g).astype(F32)
        out[pl.ds((len(off) + k) * B, B), :] = jnp.where(r <= c, first, second).astype(BF)
        rows.append(jnp.sum(jnp.where(r == c, second, 0.0), axis=0, keepdims=True))
    n_rows = out.shape[0] - aux
    if not n_rows:
        return
    rows.append(jnp.zeros((n_rows - len(rows), B), F32))
    out[pl.ds(aux, n_rows), :] = jnp.concatenate(rows, axis=0).astype(BF)


def pack_corner_kernel(x, ret, out, buf, smem, sem, ret_sem):
    flip = flip_core()
    load = pltpu.make_async_copy(ret, smem, ret_sem)
    load.start()
    blocks = A_OFF + [(h, h) for pair in A_PACK for h in pair]
    copies = {}
    for n, (h, g) in enumerate(blocks):
        row, slot = place(flip, h + 2, g - h + 4)
        copies[h, g] = (pltpu.make_async_copy(x.at[row, slot], buf.at[n], sem.at[n]), n)
        copies[h, g][0].start()
    load.wait()

    def get(h, g):
        copy, n = copies[h, g]
        copy.wait()
        m = jnp.full((16, B), smem_mask(smem, flip, h + 2, g + 2), F32).astype(BF)
        return buf[n] * whole(m)

    def mask_of(h, g):
        return jnp.full((1, B), smem_mask(smem, flip, h + 2, g + 2), F32)

    send_rows(out, A_OFF, A_PACK, MASKS, get, mask_of)


def pack_corner(x, ret):
    n = len(A_OFF) + 2 * len(A_PACK)
    return pl.pallas_call(
        pack_corner_kernel,
        out_shape=jax.ShapeDtypeStruct((A_ROWS, B), BF),
        in_specs=[HBM, HBM],
        out_specs=VM,
        scratch_shapes=[
            pltpu.VMEM((n, B, B), BF),
            pltpu.SMEM((R, W), jnp.int32),
            pltpu.SemaphoreType.DMA((n,)),
            pltpu.SemaphoreType.DMA,
        ],
        compiler_params=pltpu.CompilerParams(vmem_limit_bytes=4 * MIB),
        cost_estimate=pl.CostEstimate(flops=1000, bytes_accessed=MIB, transcendentals=0),
        name="pack_corner",
    )(x, ret)


MK = R * W + 6


def pack_deep_body(x, ret, pb, pc, xin, mk, smem, sem, ret_sem):
    flip = flip_core()
    load = pltpu.make_async_copy(ret, smem, ret_sem)
    load.start()
    copies = {}
    for i in [*range(2, R), 0, 1]:
        row, _ = place(flip, i, 0)
        copies[i] = pltpu.make_async_copy(x.at[row], xin.at[i], sem.at[i])
        copies[i].start()
    load.wait()
    for i in range(R):
        for w in range(W):
            mk[pl.ds(i * W + w, 1), :] = jnp.full((1, B), smem_mask(smem, flip, i, i + w - 4), F32)
    mk[pl.ds(R * W, MK - R * W), :] = jnp.zeros((MK - R * W, B), F32)
    for i in range(2, R):
        copies[i].wait()

    def get(h, g):
        _, slot = place(flip, h + 2, g - h + 4)
        m = jnp.full((16, B), smem_mask(smem, flip, h + 2, g + 2), F32).astype(BF)
        return xin[h + 2, slot] * whole(m)

    send_rows(pb, B_OFF, [], [], get, None)
    send_rows(pc, C_OFF, C_PACK, [], get, None)
    copies[0].wait()
    copies[1].wait()


CORNER = [(r, c) for r in range(6, 9) for c in range(6, 9)]
CUT = 5


def put_swap(store, swap_a, swap_b, I, J):
    def both(a, b, v):
        store(a, b, v)
        at = (R - 1 - 2 * I - a, R - 1 - 2 * J - b)
        if at in CORNER:
            n = CORNER.index(at)
            if n < CUT:
                swap_a[n] = v
            else:
                swap_b[n - CUT] = v

    return both


D1_EARLY = [(0, 2), (2, 0), (1, 2), (2, 1), (2, 2), (1, 3), (3, 1), (2, 3), (3, 2), (2, 4), (4, 2)]
D1_CORNER = [(0, 0), (0, 1), (1, 0), (1, 1)]
S_EARLY = [(I, J) for I in range(5) for J in range(I, min(I + 3, 5))]
D1 = jax.ShapeDtypeStruct((7, 5 * T, T), BF)
HROWS = jax.ShapeDtypeStruct((4, T, 5 * T), BF)


def xh_at(I, J):
    return (I + 4, slice(None), pl.ds((J - I + 2) * T, T))


def sb_at(I, J):
    return (I + 2, slice(None), pl.ds((J - I + 2) * T, T))


def sb_store(sb, I, J):
    def store(a, b, v):
        sb[I + 2, pl.ds(a * B, B), pl.ds((J - I + 2) * T + b * B, B)] = v

    return store


def rows_of(xb01, xh):
    def xs(I, lo, hi):
        cols = pl.ds((lo - I + 2) * T, (hi - lo + 1) * T)
        return xb01[I, :, cols] if I >= 0 else xh[I + 4, :, cols]

    return xs


def square_rows(sb):
    def ss(I, lo, hi):
        return sb[I + 2, :, pl.ds((lo - I + 2) * T, (hi - lo + 1) * T)]

    return ss


def own_masks(mk):
    def mask(i, j):
        i, w = own_slot(i, j)
        return mk[pl.ds(i * W + w, 1), :]

    return mask


def early_body(xin, mk, xb01, xh, sb, acc, d1, xb, s):
    flip = flip_core()
    mask = own_masks(mk)

    for I in range(5):
        xb[I, pl.ds(0, B), pl.ds(9 * B, B)] = jnp.zeros((B, B), BF)
        xb[I, pl.ds(B, B), pl.ds(0, B)] = jnp.zeros((B, B), BF)
        for a in range(2):
            i = 2 * I + a
            for w in range(W):
                _, slot = place(flip, i, w)
                m = jnp.broadcast_to(mask(i, i + w - 4), (16, B)).astype(BF)
                v = xin[i, slot] * whole(m)
                xb[I, pl.ds(a * B, B), pl.ds((a + w) * B, B)] = v
                if I < 2:
                    xb01[I, pl.ds(a * B, B), pl.ds((a + w) * B, B)] = v
        if I < 2:
            xb01[I, pl.ds(0, B), pl.ds(9 * B, B)] = jnp.zeros((B, B), BF)
            xb01[I, pl.ds(B, B), pl.ds(0, B)] = jnp.zeros((B, B), BF)

    def xs(I, lo, hi):
        return xb[I, :, pl.ds((lo - I + 2) * T, (hi - lo + 1) * T)]

    def ss(I, lo, hi):
        return s[I, :, pl.ds((lo - I + 2) * T, (hi - lo + 1) * T)]

    one = eye()
    for I, K in S_CROSS:
        xh[xh_at(K, I)] = nt(one, xs(I, K, K)).astype(BF)

    for I, J in S_EARLY:
        def store(a, b, v, I=I, J=J):
            s[I, pl.ds(a * B, B), pl.ds((J - I + 2) * T + b * B, B)] = v

        put_masked(store, nt(xs(I, J - 2, I + 2), xs(J, J - 2, I + 2)), I, J, mask)
        if I < J:
            s[J, :, pl.ds((I - J + 2) * T, T)] = nt(one, ss(I, J, J)).astype(BF)

    for n, (I, J) in enumerate(D1_CORNER):
        sb[sb_at(I, J)] = ss(I, J, J)
        lo, hi = max(0, I - 2, J - 2), min(I, J) + 2
        acc[n] = nt(ss(I, lo, hi), xs(J, lo, hi))

    for I, J in D1_EARLY:
        lo, hi = max(I, J) - 2, min(I, J) + 2
        put_step(d1_store(d1, I, J), xs(I, J, J), nt(ss(I, lo, hi), xs(J, lo, hi)), I, J, mask)


PB = jax.ShapeDtypeStruct((B_ROWS, B), BF)
PC = jax.ShapeDtypeStruct((C_ROWS, B), BF)
XIN = jax.ShapeDtypeStruct((R, W, B, B), BF)
MASK_ROWS = jax.ShapeDtypeStruct((MK, B), F32)
EARLY = [
    jax.ShapeDtypeStruct((2, T, 5 * T), BF),
    HROWS,
    HROWS,
    jax.ShapeDtypeStruct((4, T, T), F32),
    D1,
]
DEEP_SCRATCH = [
    pltpu.SMEM((R, W), jnp.int32),
    pltpu.SemaphoreType.DMA((R,)),
    pltpu.SemaphoreType.DMA,
]
EARLY_SCRATCH = [pltpu.VMEM((5, T, 5 * T), BF), pltpu.VMEM((5, T, 5 * T), BF)]


AHEAD = 5


def goes_ahead():
    return jnp.logical_and(lax.axis_index("grid") < AHEAD, flip_core() == 1)


def ahead_kernel(x, ret, pa_in, pa, pb, pc, xin, mk, *refs):
    del pa_in, pa
    outs, scratch = refs[: len(EARLY)], refs[len(EARLY) :]

    @pl.when(goes_ahead())
    def _():
        pack_deep_body(x, ret, pb, pc, xin, mk, *scratch[2:])
        early_body(xin, mk, *outs, *scratch[:2])


def ahead(x, ret, pa):
    return pl.pallas_call(
        ahead_kernel,
        out_shape=[jax.ShapeDtypeStruct((A_ROWS, B), BF), PB, PC, XIN, MASK_ROWS, *EARLY],
        in_specs=[HBM, HBM, VM],
        out_specs=[VM] * (5 + len(EARLY)),
        scratch_shapes=EARLY_SCRATCH + DEEP_SCRATCH,
        input_output_aliases={2: 0},
        compiler_params=pltpu.CompilerParams(vmem_limit_bytes=24 * MIB),
        cost_estimate=pl.CostEstimate(flops=1000, bytes_accessed=1000, transcendentals=0),
        name="ahead",
    )(x, ret, pa)


def pack_deep_kernel(x, ret, *refs):
    @pl.when(jnp.logical_not(goes_ahead()))
    def _():
        pack_deep_body(x, ret, *refs[4:])


def pack_deep(x, ret, pb, pc, xin, mk):
    return pl.pallas_call(
        pack_deep_kernel,
        out_shape=[PB, PC, XIN, MASK_ROWS],
        in_specs=[HBM, HBM, VM, VM, VM, VM],
        out_specs=[VM] * 4,
        scratch_shapes=DEEP_SCRATCH,
        input_output_aliases={2: 0, 3: 1, 4: 2, 5: 3},
        compiler_params=pltpu.CompilerParams(vmem_limit_bytes=8 * MIB),
        cost_estimate=pl.CostEstimate(flops=1000, bytes_accessed=4 * MIB, transcendentals=0),
        name="pack_deep",
    )(x, ret, pb, pc, xin, mk)


def early_kernel(xin, mk, *refs):
    @pl.when(jnp.logical_not(goes_ahead()))
    def _():
        early_body(xin, mk, *refs[len(EARLY) :])


def early(xin, mk, *outs):
    return pl.pallas_call(
        early_kernel,
        out_shape=EARLY,
        in_specs=[VM] * (2 + len(EARLY)),
        out_specs=[VM] * len(EARLY),
        scratch_shapes=EARLY_SCRATCH,
        input_output_aliases={2 + n: n for n in range(len(EARLY))},
        compiler_params=pltpu.CompilerParams(vmem_limit_bytes=24 * MIB),
        cost_estimate=pl.CostEstimate(flops=2 * T * T * T, bytes_accessed=1000, transcendentals=0),
        name="early",
    )(xin, mk, *outs)


def halo_mask(mk, pa):
    own = own_masks(mk)

    def mask(i, j):
        if 0 <= i < R or 0 <= j < R:
            return own(i, j)
        n = MASKS.index((max(i, j) + 8, min(i, j) + 8))
        return pa[pl.ds(NA * B + n, 1), :].astype(F32)

    return mask


def unpack(ref, off, packs, base, aux, xh, one):
    r, c_ = iotas(B)
    n_off = len(off)

    def dst(h, c):
        I, J = h // 2 - 4, c // 2 - 4
        return (I + 4, pl.ds((h % 2) * B, B), pl.ds((J - I + 2) * T + (c % 2) * B, B))

    tiles = set()
    for n, (h, c) in enumerate(off):
        xh[dst(h, c)] = ref[pl.ds(n * B, B), :]
        if h // 2 == c // 2:
            xh[dst(c, h)] = nt(one[:B, :B], ref[pl.ds(n * B, B), :]).astype(BF)
        else:
            tiles.add((h // 2 - 4, c // 2 - 4))
    for k, (h, g) in enumerate(packs):
        both = ref[pl.ds((base + k) * B, B), :]
        turned = nt(one[:B, :B], both)
        both = both.astype(F32)
        xh[dst(h, h)] = jnp.where(r <= c_, both, turned).astype(BF)
        other = jnp.where(r < c_, turned, both)
        diagonal = ref[pl.ds(aux + k, 1), :].astype(F32)
        xh[dst(g, g)] = jnp.where(r == c_, diagonal, other).astype(BF)
    for I, J in sorted(tiles):
        for a in range(2):
            for b in range(2):
                if abs(2 * I + a - 2 * J - b) > 4:
                    xh[dst(2 * I + a + 8, 2 * J + b + 8)] = jnp.zeros((B, B), BF)
        xh[xh_at(J, I)] = nt(one, xh[xh_at(I, J)]).astype(BF)


S_CROSS = [(0, -2), (0, -1), (1, -1)]
def corner_kernel(pa, xb01, acc, mk, xh_in, sb_in, d1_in, xh, sb, d1, swap_a, swap_b):
    del xh_in, sb_in, d1_in
    mask = halo_mask(mk, pa)
    one = eye()
    unpack(pa, A_OFF, A_PACK, len(A_OFF), NA * B + len(MASKS), xh, one)
    xs = rows_of(xb01, xh)
    ss = square_rows(sb)

    for I, J in S_CROSS:
        put_masked(sb_store(sb, I, J), nt(xs(I, I - 2, J + 2), xs(J, I - 2, J + 2)), I, J, mask)
    terms = {(0, 0): -2, (0, 1): -1, (1, 0): -1, (1, 1): -1}
    for n, (I, J) in enumerate(D1_CORNER):
        lo = terms[I, J]
        cube = acc[n] + nt(ss(I, lo, -1), xs(J, lo, -1))
        store = put_swap(d1_store(d1, I, J), swap_a, swap_b, I, J)
        put_step(store, xs(I, J, J), cube, I, J, mask)
    for I, J in S_CROSS:
        cube = nt(ss(I, I - 2, J + 2), xs(J, I - 2, J + 2))
        put_step(d1_store(d1, I, J), xs(I, J, J), cube, I, J, mask)


def corner(pa, xb01, acc, mk, xh, sb, d1):
    return pl.pallas_call(
        corner_kernel,
        out_shape=[
            HROWS,
            HROWS,
            D1,
            jax.ShapeDtypeStruct((CUT, B, B), BF),
            jax.ShapeDtypeStruct((len(CORNER) - CUT, B, B), BF),
        ],
        in_specs=[VM] * 7,
        out_specs=[VM] * 5,
        input_output_aliases={4: 0, 5: 1, 6: 2},
        compiler_params=pltpu.CompilerParams(vmem_limit_bytes=16 * MIB),
        cost_estimate=pl.CostEstimate(flops=2 * 32 * T * T * T, bytes_accessed=1000, transcendentals=0),
        name="corner",
    )(pa, xb01, acc, mk, xh, sb, d1)


H = R // 2
Q = 2 * SHARE
M = H * Q
S_PART = [(-1, -1), (-2, -2), (-1, -2)]
D1_HALO = [(-2, 0), (-1, 0), (-1, 1), (-1, -1), (-1, -2), (-2, -1), (-2, -2)]
LEFT = jax.ShapeDtypeStruct((M, 7 * T), BF)


def chip_share():
    layer = lax.axis_index("layer")
    return lax.rem(layer, 2), pl.multiple_of(lax.div(layer, 2) * Q, Q)


def in_rows(J):
    return max(0, 2 * J - 4), min(H - 1, 2 * J + 5)


def put_left(left, d1, i, J, chip_rows):
    I, a = i // 2, i % 2
    dst = (pl.ds(i * Q, Q), pl.ds((J + 2) * T, T))
    if abs(I - J) <= 2:
        left[dst] = d1[J + 2, pl.ds((I - J + 2) * T + a * B + chip_rows, Q), :]
    else:
        left[dst] = jnp.zeros((Q, T), BF)


def product(lhs, d1, J, i0, i1, k0, k1):
    a = lhs[pl.ds(i0 * Q, (i1 - i0 + 1) * Q), pl.ds((k0 + 2) * T, (k1 - k0 + 1) * T)]
    return nn(a, d1[J + 2, pl.ds((k0 - J + 2) * T, (k1 - k0 + 1) * T), :])


def beside_kernel(xb01, mk, xh, sb, d1_in, d1, left, sp, xp, s1p):
    del mk, d1_in
    _, chip_rows = chip_share()
    one = eye()
    xs = rows_of(xb01, xh)

    def ss(I, m):
        return nt(one, sb[sb_at(m, I)]).astype(BF)

    turned = {(-2, 0): ss(-2, 0), (-1, 0): ss(-1, 0), (-1, 1): ss(-1, 1)}
    for n, (I, J) in enumerate(S_PART):
        sp[n] = nt(xs(I, -2, J + 2 if I >= J else I + 2), xs(J, -2, J + 2 if I >= J else I + 2))
    for n, (I, J) in enumerate(D1_HALO):
        total = None
        for m in range(min(I, J) + 3):
            term = nt(turned[I, m], xs(J, m, m))
            total = term if total is None else total + term
        xp[n] = total
    for i in range(H):
        for J in range(-2, 5):
            put_left(left, d1, i, J, chip_rows)
    for J, k1 in [(-2, 0), (-1, 1), (0, 2)]:
        i0, i1 = in_rows(J)
        s1p[pl.ds(i0 * Q, (i1 - i0 + 1) * Q), pl.ds((J + 2) * T, T)] = product(left, d1, J, i0, i1, 0, k1)


def beside(xb01, mk, xh, sb, d1):
    return pl.pallas_call(
        beside_kernel,
        out_shape=[
            D1,
            LEFT,
            jax.ShapeDtypeStruct((len(S_PART), T, T), F32),
            jax.ShapeDtypeStruct((len(D1_HALO), T, T), F32),
            jax.ShapeDtypeStruct((M, 3 * T), F32),
        ],
        in_specs=[VM] * 5,
        out_specs=[VM] * 5,
        input_output_aliases={4: 0},
        compiler_params=pltpu.CompilerParams(vmem_limit_bytes=16 * MIB),
        cost_estimate=pl.CostEstimate(flops=1000, bytes_accessed=1000, transcendentals=0),
        name="beside",
    )(xb01, mk, xh, sb, d1)


def put_square(s1, s, J, i0, mask):
    i1 = i0 + s.shape[0] // Q - 1
    for i in range(H):
        for b in range(2):
            j = 2 * J + b
            dst = (pl.ds(i * Q, Q), pl.ds((J + 2) * T + b * B, B))
            if abs(i - j) <= 4:
                assert i0 <= i <= i1
                q = s[(i - i0) * Q : (i - i0 + 1) * Q, b * B : (b + 1) * B]
                s1[dst] = (q * mask(i, j)).astype(BF)
            else:
                s1[dst] = jnp.zeros((Q, B), BF)


def swapped_kernel(swap_a, swap_b, mk, left, d1_in, d1, s1, s1q, x2p):
    del d1_in
    mask = own_masks(mk)

    def put(r, c, v):
        d1_store(d1, r // 2, c // 2)(r % 2, c % 2, v)

    for n, (r, c) in enumerate(CORNER):
        put(r, c, swap_a[n] if n < CUT else swap_b[n - CUT])
    for k in range(6, R):
        put(k, R - 1, jnp.zeros((B, B), BF))
        if k < R - 1:
            put(R - 1, k, jnp.zeros((B, B), BF))
    for J in (2, 3, 4):
        i0, i1 = in_rows(J)
        put_square(s1, product(left, d1, J, i0, i1, max(J - 2, 0), 4), J, i0, mask)
    s1q[...] = product(left, d1, 1, 0, H - 1, 0, 3)
    for J in range(5):
        i0, i1 = in_rows(J)
        part = product(s1, d1, J, i0, i1, 2, min(J + 2, 4))
        x2p[pl.ds(i0 * Q, (i1 - i0 + 1) * Q), pl.ds(J * T, T)] = part


def use_swapped(swap_a, swap_b, mk, left, d1):
    return pl.pallas_call(
        swapped_kernel,
        out_shape=[D1, LEFT, jax.ShapeDtypeStruct((M, T), F32), jax.ShapeDtypeStruct((M, 5 * T), F32)],
        in_specs=[VM] * 5,
        out_specs=[VM] * 4,
        input_output_aliases={4: 0},
        compiler_params=pltpu.CompilerParams(vmem_limit_bytes=16 * MIB),
        cost_estimate=pl.CostEstimate(flops=1000, bytes_accessed=1000, transcendentals=0),
        name="use_swapped",
    )(swap_a, swap_b, mk, left, d1)


S_DEEP = [(-1, -3), (-2, -3), (-2, -4)]
D1_DEEP = [(-1, -1), (-1, -2), (-2, -1), (-2, -2)]
HALF = jax.ShapeDtypeStruct((H, W, SHARE, B), BF)
X2C = jax.ShapeDtypeStruct((M, 4 * T), F32)


def emit(keep, send, flip, left, mask, J, i0, cube):
    for i in range(i0, i0 + cube.shape[0] // Q):
        for b in range(2):
            j = 2 * J + b
            if abs(i - j) > 4:
                continue
            q = cube[(i - i0) * Q : (i - i0 + 1) * Q, b * B : (b + 1) * B] * mask(i, j)
            x = left[pl.ds(i * Q, Q), pl.ds((J + 2) * T + b * B, B)].astype(F32)
            v = (3.0 * x - q * SCALE) * 0.5
            w = j - i + 4
            near = jnp.where(flip == 1, H - 1 - i, i)
            slot = jnp.where(flip == 1, W - 1 - w, w)
            lo, hi = v[:SHARE].astype(BF), v[SHARE:].astype(BF)
            keep[near, slot] = jnp.where(flip == 1, hi, lo)
            send[near, slot] = jnp.where(flip == 1, lo, hi)


def plus(part, i0, whole_ref, cols, j0, j1):
    n = part.shape[0] // Q
    assert j0 == i0
    total = part + whole_ref[pl.ds(i0 * Q, n * Q), cols]
    if j1 >= i0 + n:
        total = jnp.concatenate([total, whole_ref[pl.ds((i0 + n) * Q, (j1 - i0 - n + 1) * Q), cols]], axis=0)
    return total


def middle_kernel(pa, pb, xb01, mk, left, sp, xp, s1p, s1q, x2p, xh_in, sb_in, d1_in, s1_in, *outs):
    del xh_in, sb_in, d1_in, s1_in
    xh, sb, d1, s1, sdp, xc, x2c, keep, send = outs
    flip, _ = chip_share()
    mask = halo_mask(mk, pa)
    one = eye()
    unpack(pb, B_OFF, [], 0, 0, xh, one)
    xs = rows_of(xb01, xh)
    ss = square_rows(sb)

    for n, (I, J) in enumerate(S_PART):
        lo = max(I, J) - 2
        put_masked(sb_store(sb, I, J), sp[n] + nt(xs(I, lo, -3), xs(J, lo, -3)), I, J, mask)
    sb[sb_at(-2, -1)] = nt(one, ss(-1, -2, -2)).astype(BF)
    for n, (I, J) in enumerate(S_DEEP):
        sdp[n] = nt(xs(I, -2, J + 2), xs(J, -2, J + 2))
    for n, (I, J) in enumerate(D1_HALO):
        lo = max(I, J) - 2
        total = xp[n] + nt(ss(I, max(lo, -2), -1), xs(J, max(lo, -2), -1))
        if (I, J) in D1_DEEP:
            xc[D1_DEEP.index((I, J))] = total
        else:
            put_step(d1_store(d1, I, J), xs(I, J, J), total, I, J, mask)

    part = product(left, d1, 1, 0, 3, -1, -1)
    put_square(s1, plus(part, 0, s1q, pl.ds(0, T), 0, 4), 1, 0, mask)
    part = product(left, d1, 0, 0, 3, -2, -1)
    put_square(s1, plus(part, 0, s1p, pl.ds(2 * T, T), 0, 4), 0, 0, mask)

    for J in range(4, -3, -1):
        i0, i1 = in_rows(J)
        rows = pl.ds(i0 * Q, (i1 - i0 + 1) * Q)
        if J == 4:
            total = x2p[rows, pl.ds(J * T, T)]
        else:
            total = product(s1, d1, J, i0, i1, max(J - 2, 0), min(J + 2, 1))
            if J >= 0:
                total = total + x2p[rows, pl.ds(J * T, T)]
        if J >= 2:
            emit(keep, send, flip, left, mask, J, i0, total)
        else:
            x2c[rows, pl.ds((J + 2) * T, T)] = total


def middle(pa, pb, xb01, mk, left, sp, xp, s1p, s1q, x2p, xh, sb, d1, s1):
    return pl.pallas_call(
        middle_kernel,
        out_shape=[
            HROWS,
            HROWS,
            D1,
            LEFT,
            jax.ShapeDtypeStruct((len(S_DEEP), T, T), F32),
            jax.ShapeDtypeStruct((len(D1_DEEP), T, T), F32),
            X2C,
            HALF,
            HALF,
        ],
        in_specs=[VM] * 14,
        out_specs=[VM] * 9,
        input_output_aliases={10: 0, 11: 1, 12: 2, 13: 3},
        compiler_params=pltpu.CompilerParams(vmem_limit_bytes=16 * MIB),
        cost_estimate=pl.CostEstimate(flops=1000, bytes_accessed=1000, transcendentals=0),
        name="middle",
    )(pa, pb, xb01, mk, left, sp, xp, s1p, s1q, x2p, xh, sb, d1, s1)


def finish_kernel(pa, pc, xb01, mk, left, s1p, sdp, xc, x2c, *refs):
    xh, sb, d1, s1, keep, send = refs[6:]
    flip, _ = chip_share()
    mask = halo_mask(mk, pa)
    unpack(pc, C_OFF, C_PACK, len(C_OFF), NC * B, xh, eye())
    xs = rows_of(xb01, xh)
    ss = square_rows(sb)

    for n, (I, J) in enumerate(S_DEEP):
        lo = I - 2
        put_masked(sb_store(sb, I, J), sdp[n] + nt(xs(I, lo, -3), xs(J, lo, -3)), I, J, mask)
    for n, (I, J) in enumerate(D1_DEEP):
        lo = max(I, J) - 2
        put_step(d1_store(d1, I, J), xs(I, J, J), xc[n] + nt(ss(I, lo, -3), xs(J, lo, -3)), I, J, mask)
    for J in (-1, -2):
        i0, i1 = in_rows(J)
        part = product(left, d1, J, i0, i1, -2, -1)
        put_square(s1, part + s1p[pl.ds(i0 * Q, (i1 - i0 + 1) * Q), pl.ds((J + 2) * T, T)], J, i0, mask)
    for J in (1, 0, -1, -2):
        i0, i1 = in_rows(J)
        part = product(s1, d1, J, i0, min(i1, 3), max(J - 2, -2), -1)
        emit(keep, send, flip, left, mask, J, i0, plus(part, i0, x2c, pl.ds((J + 2) * T, T), i0, i1))


def finish(pa, pc, xb01, mk, left, s1p, sdp, xc, x2c, xh, sb, d1, s1, keep, send):
    return pl.pallas_call(
        finish_kernel,
        out_shape=[HROWS, HROWS, D1, LEFT, HALF, HALF],
        in_specs=[VM] * 15,
        out_specs=[VM] * 6,
        input_output_aliases={9 + n: n for n in range(6)},
        compiler_params=pltpu.CompilerParams(vmem_limit_bytes=16 * MIB),
        cost_estimate=pl.CostEstimate(flops=2 * 30 * T * T * T, bytes_accessed=4 * MIB, transcendentals=0),
        name="finish",
    )(pa, pc, xb01, mk, left, s1p, sdp, xc, x2c, xh, sb, d1, s1, keep, send)


def half_out(src, out, sem, first):
    copies = []
    for n in range(H):
        copies.append(pltpu.make_async_copy(src.at[n], out.at[first + n], sem.at[n]))
        copies[-1].start()
    for copy in copies:
        copy.wait()


def keep_kernel(keep, out, sem):
    half_out(keep, out, sem, jnp.where(flip_core() == 1, H, 0))


def join_kernel(other, out_in, out, sem):
    del out_in
    half_out(other, out, sem, jnp.where(flip_core() == 1, 0, H))


OUT = jax.ShapeDtypeStruct((R, W, SHARE, B), BF)


def put_keep(keep):
    return pl.pallas_call(
        keep_kernel,
        out_shape=OUT,
        in_specs=[VM],
        out_specs=HBM,
        scratch_shapes=[pltpu.SemaphoreType.DMA((H,))],
        compiler_params=pltpu.CompilerParams(vmem_limit_bytes=2 * MIB),
        cost_estimate=pl.CostEstimate(flops=1000, bytes_accessed=1000, transcendentals=0),
        name="put_keep",
    )(keep)


def join(other, out):
    return pl.pallas_call(
        join_kernel,
        out_shape=OUT,
        in_specs=[VM, HBM],
        out_specs=HBM,
        scratch_shapes=[pltpu.SemaphoreType.DMA((H,))],
        input_output_aliases={1: 0},
        compiler_params=pltpu.CompilerParams(vmem_limit_bytes=2 * MIB),
        name="join",
    )(other, out)


def chain(layers, grid):
    pairs = []
    for l in range(layers):
        for g in range(grid):
            pairs.append((l * grid + g, l * grid + (g + 1 if l % 2 == 0 else g - 1) % grid))
    return pairs


def per_device(x, ret):
    layers, grid = lax.axis_size("layer"), lax.axis_size("grid")
    cores = [(l, l ^ 1) for l in range(layers)]
    pairs = chain(layers, grid)
    x = pltpu.with_memory_space_constraint(x, pltpu.HBM)
    ret = pltpu.with_memory_space_constraint(ret, pltpu.HBM)
    pa, pb, pc, xin, mk, *outs = ahead(x, ret, pack_corner(x, ret))
    pa = lax.ppermute(pa, ("layer", "grid"), pairs)
    pb, pc, xin, mk = pack_deep(x, ret, pb, pc, xin, mk)
    pb = lax.ppermute(pb, ("layer", "grid"), pairs)
    pc = lax.ppermute(pc, ("layer", "grid"), pairs)
    xb01, xh, sb, acc, d1 = early(xin, mk, *outs)
    xh, sb, d1, swap_a, swap_b = corner(pa, xb01, acc, mk, xh, sb, d1)
    swap_a = lax.ppermute(swap_a, "layer", cores)
    swap_b = lax.ppermute(swap_b, "layer", cores)
    d1, left, sp, xp, s1p = beside(xb01, mk, xh, sb, d1)
    d1, s1, s1q, x2p = use_swapped(swap_a, swap_b, mk, left, d1)
    xh, sb, d1, s1, sdp, xc, x2c, keep, send = middle(
        pa, pb, xb01, mk, left, sp, xp, s1p, s1q, x2p, xh, sb, d1, s1
    )
    *_, keep, send = finish(pa, pc, xb01, mk, left, s1p, sdp, xc, x2c, xh, sb, d1, s1, keep, send)
    other = lax.ppermute(send, "layer", cores)
    return join(other, put_keep(keep))


def solution(mesh):
    return jax.shard_map(
        per_device,
        mesh=mesh,
        in_specs=(P("grid", None, None, None), P("grid", None)),
        out_specs=P("grid", None, "layer", None),
        check_vma=False,
    )
```

```python
import jax
import jax.numpy as jnp
from jax import lax
from jax.experimental import pallas as pl
from jax.experimental.pallas import tpu as pltpu
from jax.sharding import PartitionSpec as P

B = 128
T = 256
R = 10
W = 9
SHARE = 32
SCALE = 1.0 / (4.0 * W * B)
BF = jnp.bfloat16
F32 = jnp.float32
MIB = 2**20

A_OFF = [(5, 4), (6, 4), (7, 4), (6, 5), (7, 5), (7, 6)]
A_PACK = [(4, 5), (6, 7)]
A_PAIRS = [(h, c) for h in range(4, 8) for c in range(4, h + 1)]
B_OFF = [(h, c) for h in range(4, 8) for c in range(h - 4, 4)]
C_OFF = [(h - 4, c - 4) for h, c in A_OFF]
C_PACK = [(h - 4, c - 4) for h, c in A_PACK]
MASKS = A_PAIRS + B_OFF
NA = len(A_OFF) + 2
NC = len(C_OFF) + 2
A_ROWS = NA * B + 32
B_ROWS = len(B_OFF) * B
C_ROWS = NC * B + 16

HBM = pl.BlockSpec(memory_space=pltpu.HBM)
VM = pl.BlockSpec(memory_space=pltpu.VMEM)


def nt(a, b):
    return lax.dot_general(a, b, (((1,), (1,)), ((), ())), preferred_element_type=F32)


def nn(a, b):
    return lax.dot_general(a, b, (((1,), (0,)), ((), ())), preferred_element_type=F32)


def flip_core():
    return lax.rem(lax.axis_index("layer"), 2)


def place(flip, i, w):
    return jnp.where(flip == 1, R - 1 - i, i), jnp.where(flip == 1, W - 1 - w, w)


def own_slot(i, j):
    if not 0 <= i < R:
        i, j = j, i
    return i, j - i + 4


def smem_mask(ret, flip, i, j):
    row, slot = place(flip, *own_slot(i, j))
    return (ret[row, slot] != 0).astype(F32)


def iotas(n):
    return lax.broadcasted_iota(jnp.int32, (n, n), 0), lax.broadcasted_iota(jnp.int32, (n, n), 1)


def eye():
    r, c = iotas(T)
    return (r == c).astype(F32).astype(BF)


def whole(row16):
    return jnp.concatenate([row16] * (B // 16), axis=0)


def put_masked(store, tile, I, J, mask):
    for a in range(2):
        for b in range(2):
            i, j = 2 * I + a, 2 * J + b
            if abs(i - j) > 4:
                store(a, b, jnp.zeros((B, B), BF))
            else:
                store(a, b, (tile[a * B : (a + 1) * B, b * B : (b + 1) * B] * mask(i, j)).astype(BF))


def put_step(store, x, cube, I, J, mask):
    for a in range(2):
        for b in range(2):
            i, j = 2 * I + a, 2 * J + b
            if abs(i - j) > 4:
                store(a, b, jnp.zeros((B, B), BF))
            else:
                q = cube[a * B : (a + 1) * B, b * B : (b + 1) * B] * mask(i, j)
                xq = x[a * B : (a + 1) * B, b * B : (b + 1) * B].astype(F32)
                store(a, b, ((3.0 * xq - q * SCALE) * 0.5).astype(BF))


def at(ref, *lead):
    def store(a, b, v):
        ref[(*lead, pl.ds(a * B, B), pl.ds(b * B, B))] = v

    return store


def d1_store(d1, I, J):
    def store(a, b, v):
        d1[J + 2, pl.ds((I - J + 2) * T + a * B, B), pl.ds(b * B, B)] = v

    return store


def send_rows(out, off, packs, masks, get, mask_of):
    r, c = iotas(B)
    aux = (len(off) + len(packs)) * B
    for n, (h, g) in enumerate(off):
        out[pl.ds(n * B, B), :] = get(h, g)
    rows = [mask_of(h, g) for h, g in masks]
    for k, (h, g) in enumerate(packs):
        first, second = get(h, h).astype(F32), get(g, g).astype(F32)
        out[pl.ds((len(off) + k) * B, B), :] = jnp.where(r <= c, first, second).astype(BF)
        rows.append(jnp.sum(jnp.where(r == c, second, 0.0), axis=0, keepdims=True))
    n_rows = out.shape[0] - aux
    if not n_rows:
        return
    rows.append(jnp.zeros((n_rows - len(rows), B), F32))
    out[pl.ds(aux, n_rows), :] = jnp.concatenate(rows, axis=0).astype(BF)


def pack_corner_kernel(x, ret, out, buf, smem, sem, ret_sem):
    flip = flip_core()
    load = pltpu.make_async_copy(ret, smem, ret_sem)
    load.start()
    blocks = A_OFF + [(h, h) for pair in A_PACK for h in pair]
    copies = {}
    for n, (h, g) in enumerate(blocks):
        row, slot = place(flip, h + 2, g - h + 4)
        copies[h, g] = (pltpu.make_async_copy(x.at[row, slot], buf.at[n], sem.at[n]), n)
        copies[h, g][0].start()
    load.wait()

    def get(h, g):
        copy, n = copies[h, g]
        copy.wait()
        m = jnp.full((16, B), smem_mask(smem, flip, h + 2, g + 2), F32).astype(BF)
        return buf[n] * whole(m)

    def mask_of(h, g):
        return jnp.full((1, B), smem_mask(smem, flip, h + 2, g + 2), F32)

    send_rows(out, A_OFF, A_PACK, MASKS, get, mask_of)


def pack_corner(x, ret):
    n = len(A_OFF) + 2 * len(A_PACK)
    return pl.pallas_call(
        pack_corner_kernel,
        out_shape=jax.ShapeDtypeStruct((A_ROWS, B), BF),
        in_specs=[HBM, HBM],
        out_specs=VM,
        scratch_shapes=[
            pltpu.VMEM((n, B, B), BF),
            pltpu.SMEM((R, W), jnp.int32),
            pltpu.SemaphoreType.DMA((n,)),
            pltpu.SemaphoreType.DMA,
        ],
        compiler_params=pltpu.CompilerParams(vmem_limit_bytes=4 * MIB),
        cost_estimate=pl.CostEstimate(flops=1000, bytes_accessed=MIB, transcendentals=0),
        name="pack_corner",
    )(x, ret)


MK = R * W + 6


def pack_deep_body(x, ret, pb, pc, xin, mk, smem, sem, ret_sem):
    flip = flip_core()
    load = pltpu.make_async_copy(ret, smem, ret_sem)
    load.start()
    copies = {}
    for i in [*range(2, R), 0, 1]:
        row, _ = place(flip, i, 0)
        copies[i] = pltpu.make_async_copy(x.at[row], xin.at[i], sem.at[i])
        copies[i].start()
    load.wait()
    for i in range(R):
        for w in range(W):
            mk[pl.ds(i * W + w, 1), :] = jnp.full((1, B), smem_mask(smem, flip, i, i + w - 4), F32)
    mk[pl.ds(R * W, MK - R * W), :] = jnp.zeros((MK - R * W, B), F32)
    for i in range(2, R):
        copies[i].wait()

    def get(h, g):
        _, slot = place(flip, h + 2, g - h + 4)
        m = jnp.full((16, B), smem_mask(smem, flip, h + 2, g + 2), F32).astype(BF)
        return xin[h + 2, slot] * whole(m)

    send_rows(pb, B_OFF, [], [], get, None)
    send_rows(pc, C_OFF, C_PACK, [], get, None)
    copies[0].wait()
    copies[1].wait()


CORNER = [(r, c) for r in range(6, 9) for c in range(6, 9)]
CUT = 5


def put_swap(store, swap_a, swap_b, I, J):
    def both(a, b, v):
        store(a, b, v)
        at = (R - 1 - 2 * I - a, R - 1 - 2 * J - b)
        if at in CORNER:
            n = CORNER.index(at)
            if n < CUT:
                swap_a[n] = v
            else:
                swap_b[n - CUT] = v

    return both


D1_EARLY = [(0, 2), (2, 0), (1, 2), (2, 1), (2, 2), (1, 3), (3, 1), (2, 3), (3, 2), (2, 4), (4, 2)]
D1_CORNER = [(0, 0), (0, 1), (1, 0), (1, 1)]
S_EARLY = [(I, J) for I in range(5) for J in range(I, min(I + 3, 5))]
D1 = jax.ShapeDtypeStruct((7, 5 * T, T), BF)
HROWS = jax.ShapeDtypeStruct((4, T, 5 * T), BF)


def xh_at(I, J):
    return (I + 4, slice(None), pl.ds((J - I + 2) * T, T))


def sb_at(I, J):
    return (I + 2, slice(None), pl.ds((J - I + 2) * T, T))


def sb_store(sb, I, J):
    def store(a, b, v):
        sb[I + 2, pl.ds(a * B, B), pl.ds((J - I + 2) * T + b * B, B)] = v

    return store


def rows_of(xb01, xh):
    def xs(I, lo, hi):
        cols = pl.ds((lo - I + 2) * T, (hi - lo + 1) * T)
        return xb01[I, :, cols] if I >= 0 else xh[I + 4, :, cols]

    return xs


def square_rows(sb):
    def ss(I, lo, hi):
        return sb[I + 2, :, pl.ds((lo - I + 2) * T, (hi - lo + 1) * T)]

    return ss


def own_masks(mk):
    def mask(i, j):
        i, w = own_slot(i, j)
        return mk[pl.ds(i * W + w, 1), :]

    return mask


def early_body(xin, mk, xb01, xh, sb, acc, d1, xb, s):
    flip = flip_core()
    mask = own_masks(mk)

    for I in range(5):
        xb[I, pl.ds(0, B), pl.ds(9 * B, B)] = jnp.zeros((B, B), BF)
        xb[I, pl.ds(B, B), pl.ds(0, B)] = jnp.zeros((B, B), BF)
        for a in range(2):
            i = 2 * I + a
            for w in range(W):
                _, slot = place(flip, i, w)
                m = jnp.broadcast_to(mask(i, i + w - 4), (16, B)).astype(BF)
                v = xin[i, slot] * whole(m)
                xb[I, pl.ds(a * B, B), pl.ds((a + w) * B, B)] = v
                if I < 2:
                    xb01[I, pl.ds(a * B, B), pl.ds((a + w) * B, B)] = v
        if I < 2:
            xb01[I, pl.ds(0, B), pl.ds(9 * B, B)] = jnp.zeros((B, B), BF)
            xb01[I, pl.ds(B, B), pl.ds(0, B)] = jnp.zeros((B, B), BF)

    def xs(I, lo, hi):
        return xb[I, :, pl.ds((lo - I + 2) * T, (hi - lo + 1) * T)]

    def ss(I, lo, hi):
        return s[I, :, pl.ds((lo - I + 2) * T, (hi - lo + 1) * T)]

    one = eye()
    for I, K in S_CROSS:
        xh[xh_at(K, I)] = nt(one, xs(I, K, K)).astype(BF)

    for I, J in S_EARLY:
        def store(a, b, v, I=I, J=J):
            s[I, pl.ds(a * B, B), pl.ds((J - I + 2) * T + b * B, B)] = v

        put_masked(store, nt(xs(I, J - 2, I + 2), xs(J, J - 2, I + 2)), I, J, mask)
        if I < J:
            s[J, :, pl.ds((I - J + 2) * T, T)] = nt(one, ss(I, J, J)).astype(BF)

    for n, (I, J) in enumerate(D1_CORNER):
        sb[sb_at(I, J)] = ss(I, J, J)
        lo, hi = max(0, I - 2, J - 2), min(I, J) + 2
        acc[n] = nt(ss(I, lo, hi), xs(J, lo, hi))

    for I, J in D1_EARLY:
        lo, hi = max(I, J) - 2, min(I, J) + 2
        put_step(d1_store(d1, I, J), xs(I, J, J), nt(ss(I, lo, hi), xs(J, lo, hi)), I, J, mask)


PB = jax.ShapeDtypeStruct((B_ROWS, B), BF)
PC = jax.ShapeDtypeStruct((C_ROWS, B), BF)
XIN = jax.ShapeDtypeStruct((R, W, B, B), BF)
MASK_ROWS = jax.ShapeDtypeStruct((MK, B), F32)
EARLY = [
    jax.ShapeDtypeStruct((2, T, 5 * T), BF),
    HROWS,
    HROWS,
    jax.ShapeDtypeStruct((4, T, T), F32),
    D1,
]
DEEP_SCRATCH = [
    pltpu.SMEM((R, W), jnp.int32),
    pltpu.SemaphoreType.DMA((R,)),
    pltpu.SemaphoreType.DMA,
]
EARLY_SCRATCH = [pltpu.VMEM((5, T, 5 * T), BF), pltpu.VMEM((5, T, 5 * T), BF)]


AHEAD = 5


def goes_ahead():
    return jnp.logical_and(lax.axis_index("grid") < AHEAD, flip_core() == 1)


def ahead_kernel(x, ret, pa_in, pa, pb, pc, xin, mk, *refs):
    del pa_in, pa
    outs, scratch = refs[: len(EARLY)], refs[len(EARLY) :]

    @pl.when(goes_ahead())
    def _():
        pack_deep_body(x, ret, pb, pc, xin, mk, *scratch[2:])
        early_body(xin, mk, *outs, *scratch[:2])


def ahead(x, ret, pa):
    return pl.pallas_call(
        ahead_kernel,
        out_shape=[jax.ShapeDtypeStruct((A_ROWS, B), BF), PB, PC, XIN, MASK_ROWS, *EARLY],
        in_specs=[HBM, HBM, VM],
        out_specs=[VM] * (5 + len(EARLY)),
        scratch_shapes=EARLY_SCRATCH + DEEP_SCRATCH,
        input_output_aliases={2: 0},
        compiler_params=pltpu.CompilerParams(vmem_limit_bytes=24 * MIB),
        cost_estimate=pl.CostEstimate(flops=1000, bytes_accessed=1000, transcendentals=0),
        name="ahead",
    )(x, ret, pa)


def pack_deep_kernel(x, ret, *refs):
    @pl.when(jnp.logical_not(goes_ahead()))
    def _():
        pack_deep_body(x, ret, *refs[4:])


def pack_deep(x, ret, pb, pc, xin, mk):
    return pl.pallas_call(
        pack_deep_kernel,
        out_shape=[PB, PC, XIN, MASK_ROWS],
        in_specs=[HBM, HBM, VM, VM, VM, VM],
        out_specs=[VM] * 4,
        scratch_shapes=DEEP_SCRATCH,
        input_output_aliases={2: 0, 3: 1, 4: 2, 5: 3},
        compiler_params=pltpu.CompilerParams(vmem_limit_bytes=8 * MIB),
        cost_estimate=pl.CostEstimate(flops=1000, bytes_accessed=4 * MIB, transcendentals=0),
        name="pack_deep",
    )(x, ret, pb, pc, xin, mk)


def early_kernel(xin, mk, *refs):
    @pl.when(jnp.logical_not(goes_ahead()))
    def _():
        early_body(xin, mk, *refs[len(EARLY) :])


def early(xin, mk, *outs):
    return pl.pallas_call(
        early_kernel,
        out_shape=EARLY,
        in_specs=[VM] * (2 + len(EARLY)),
        out_specs=[VM] * len(EARLY),
        scratch_shapes=EARLY_SCRATCH,
        input_output_aliases={2 + n: n for n in range(len(EARLY))},
        compiler_params=pltpu.CompilerParams(vmem_limit_bytes=24 * MIB),
        cost_estimate=pl.CostEstimate(flops=2 * T * T * T, bytes_accessed=1000, transcendentals=0),
        name="early",
    )(xin, mk, *outs)


def halo_mask(mk, pa):
    own = own_masks(mk)

    def mask(i, j):
        if 0 <= i < R or 0 <= j < R:
            return own(i, j)
        n = MASKS.index((max(i, j) + 8, min(i, j) + 8))
        return pa[pl.ds(NA * B + n, 1), :].astype(F32)

    return mask


def unpack(ref, off, packs, base, aux, xh, one):
    r, c_ = iotas(B)
    n_off = len(off)

    def dst(h, c):
        I, J = h // 2 - 4, c // 2 - 4
        return (I + 4, pl.ds((h % 2) * B, B), pl.ds((J - I + 2) * T + (c % 2) * B, B))

    tiles = set()
    for n, (h, c) in enumerate(off):
        xh[dst(h, c)] = ref[pl.ds(n * B, B), :]
        if h // 2 == c // 2:
            xh[dst(c, h)] = nt(one[:B, :B], ref[pl.ds(n * B, B), :]).astype(BF)
        else:
            tiles.add((h // 2 - 4, c // 2 - 4))
    for k, (h, g) in enumerate(packs):
        both = ref[pl.ds((base + k) * B, B), :]
        turned = nt(one[:B, :B], both)
        both = both.astype(F32)
        xh[dst(h, h)] = jnp.where(r <= c_, both, turned).astype(BF)
        other = jnp.where(r < c_, turned, both)
        diagonal = ref[pl.ds(aux + k, 1), :].astype(F32)
        xh[dst(g, g)] = jnp.where(r == c_, diagonal, other).astype(BF)
    for I, J in sorted(tiles):
        for a in range(2):
            for b in range(2):
                if abs(2 * I + a - 2 * J - b) > 4:
                    xh[dst(2 * I + a + 8, 2 * J + b + 8)] = jnp.zeros((B, B), BF)
        xh[xh_at(J, I)] = nt(one, xh[xh_at(I, J)]).astype(BF)


S_CROSS = [(0, -2), (0, -1), (1, -1)]
def corner_kernel(pa, xb01, acc, mk, xh_in, sb_in, d1_in, xh, sb, d1, swap_a, swap_b):
    del xh_in, sb_in, d1_in
    mask = halo_mask(mk, pa)
    one = eye()
    unpack(pa, A_OFF, A_PACK, len(A_OFF), NA * B + len(MASKS), xh, one)
    xs = rows_of(xb01, xh)
    ss = square_rows(sb)

    for I, J in S_CROSS:
        put_masked(sb_store(sb, I, J), nt(xs(I, I - 2, J + 2), xs(J, I - 2, J + 2)), I, J, mask)
    terms = {(0, 0): -2, (0, 1): -1, (1, 0): -1, (1, 1): -1}
    for n, (I, J) in enumerate(D1_CORNER):
        lo = terms[I, J]
        cube = acc[n] + nt(ss(I, lo, -1), xs(J, lo, -1))
        store = put_swap(d1_store(d1, I, J), swap_a, swap_b, I, J)
        put_step(store, xs(I, J, J), cube, I, J, mask)
    for I, J in S_CROSS:
        cube = nt(ss(I, I - 2, J + 2), xs(J, I - 2, J + 2))
        put_step(d1_store(d1, I, J), xs(I, J, J), cube, I, J, mask)


def corner(pa, xb01, acc, mk, xh, sb, d1):
    return pl.pallas_call(
        corner_kernel,
        out_shape=[
            HROWS,
            HROWS,
            D1,
            jax.ShapeDtypeStruct((CUT, B, B), BF),
            jax.ShapeDtypeStruct((len(CORNER) - CUT, B, B), BF),
        ],
        in_specs=[VM] * 7,
        out_specs=[VM] * 5,
        input_output_aliases={4: 0, 5: 1, 6: 2},
        compiler_params=pltpu.CompilerParams(vmem_limit_bytes=16 * MIB),
        cost_estimate=pl.CostEstimate(flops=2 * 32 * T * T * T, bytes_accessed=1000, transcendentals=0),
        name="corner",
    )(pa, xb01, acc, mk, xh, sb, d1)


H = R // 2
Q = 2 * SHARE
M = H * Q
S_PART = [(-1, -1), (-2, -2), (-1, -2)]
D1_HALO = [(-2, 0), (-1, 0), (-1, 1), (-1, -1), (-1, -2), (-2, -1), (-2, -2)]
LEFT = jax.ShapeDtypeStruct((M, 7 * T), BF)


def chip_share():
    layer = lax.axis_index("layer")
    return lax.rem(layer, 2), pl.multiple_of(lax.div(layer, 2) * Q, Q)


def in_rows(J):
    return max(0, 2 * J - 4), min(H - 1, 2 * J + 5)


def put_left(left, d1, i, J, chip_rows):
    I, a = i // 2, i % 2
    dst = (pl.ds(i * Q, Q), pl.ds((J + 2) * T, T))
    if abs(I - J) <= 2:
        left[dst] = d1[J + 2, pl.ds((I - J + 2) * T + a * B + chip_rows, Q), :]
    else:
        left[dst] = jnp.zeros((Q, T), BF)


def product(lhs, d1, J, i0, i1, k0, k1):
    a = lhs[pl.ds(i0 * Q, (i1 - i0 + 1) * Q), pl.ds((k0 + 2) * T, (k1 - k0 + 1) * T)]
    return nn(a, d1[J + 2, pl.ds((k0 - J + 2) * T, (k1 - k0 + 1) * T), :])


def beside_kernel(xb01, mk, xh, sb, d1_in, d1, left, sp, xp, s1p):
    del mk, d1_in
    _, chip_rows = chip_share()
    one = eye()
    xs = rows_of(xb01, xh)

    def ss(I, m):
        return nt(one, sb[sb_at(m, I)]).astype(BF)

    turned = {(-2, 0): ss(-2, 0), (-1, 0): ss(-1, 0), (-1, 1): ss(-1, 1)}
    for n, (I, J) in enumerate(S_PART):
        sp[n] = nt(xs(I, -2, J + 2 if I >= J else I + 2), xs(J, -2, J + 2 if I >= J else I + 2))
    for n, (I, J) in enumerate(D1_HALO):
        total = None
        for m in range(min(I, J) + 3):
            term = nt(turned[I, m], xs(J, m, m))
            total = term if total is None else total + term
        xp[n] = total
    for i in range(H):
        for J in range(-2, 5):
            put_left(left, d1, i, J, chip_rows)
    for J, k1 in [(-2, 0), (-1, 1), (0, 2)]:
        i0, i1 = in_rows(J)
        s1p[pl.ds(i0 * Q, (i1 - i0 + 1) * Q), pl.ds((J + 2) * T, T)] = product(left, d1, J, i0, i1, 0, k1)


def beside(xb01, mk, xh, sb, d1):
    return pl.pallas_call(
        beside_kernel,
        out_shape=[
            D1,
            LEFT,
            jax.ShapeDtypeStruct((len(S_PART), T, T), F32),
            jax.ShapeDtypeStruct((len(D1_HALO), T, T), F32),
            jax.ShapeDtypeStruct((M, 3 * T), F32),
        ],
        in_specs=[VM] * 5,
        out_specs=[VM] * 5,
        input_output_aliases={4: 0},
        compiler_params=pltpu.CompilerParams(vmem_limit_bytes=16 * MIB),
        cost_estimate=pl.CostEstimate(flops=1000, bytes_accessed=1000, transcendentals=0),
        name="beside",
    )(xb01, mk, xh, sb, d1)


def put_square(s1, s, J, i0, mask):
    i1 = i0 + s.shape[0] // Q - 1
    for i in range(H):
        for b in range(2):
            j = 2 * J + b
            dst = (pl.ds(i * Q, Q), pl.ds((J + 2) * T + b * B, B))
            if abs(i - j) <= 4:
                assert i0 <= i <= i1
                q = s[(i - i0) * Q : (i - i0 + 1) * Q, b * B : (b + 1) * B]
                s1[dst] = (q * mask(i, j)).astype(BF)
            else:
                s1[dst] = jnp.zeros((Q, B), BF)


def swapped_kernel(swap_a, swap_b, mk, left, d1_in, d1, s1, s1q, x2p):
    del d1_in
    mask = own_masks(mk)

    def put(r, c, v):
        d1_store(d1, r // 2, c // 2)(r % 2, c % 2, v)

    for n, (r, c) in enumerate(CORNER):
        put(r, c, swap_a[n] if n < CUT else swap_b[n - CUT])
    for k in range(6, R):
        put(k, R - 1, jnp.zeros((B, B), BF))
        if k < R - 1:
            put(R - 1, k, jnp.zeros((B, B), BF))
    for J in (2, 3, 4):
        i0, i1 = in_rows(J)
        put_square(s1, product(left, d1, J, i0, i1, max(J - 2, 0), 4), J, i0, mask)
    s1q[...] = product(left, d1, 1, 0, H - 1, 0, 3)
    for J in range(5):
        i0, i1 = in_rows(J)
        part = product(s1, d1, J, i0, i1, 2, min(J + 2, 4))
        x2p[pl.ds(i0 * Q, (i1 - i0 + 1) * Q), pl.ds(J * T, T)] = part


def use_swapped(swap_a, swap_b, mk, left, d1):
    return pl.pallas_call(
        swapped_kernel,
        out_shape=[D1, LEFT, jax.ShapeDtypeStruct((M, T), F32), jax.ShapeDtypeStruct((M, 5 * T), F32)],
        in_specs=[VM] * 5,
        out_specs=[VM] * 4,
        input_output_aliases={4: 0},
        compiler_params=pltpu.CompilerParams(vmem_limit_bytes=16 * MIB),
        cost_estimate=pl.CostEstimate(flops=1000, bytes_accessed=1000, transcendentals=0),
        name="use_swapped",
    )(swap_a, swap_b, mk, left, d1)


S_DEEP = [(-1, -3), (-2, -3), (-2, -4)]
D1_DEEP = [(-1, -1), (-1, -2), (-2, -1), (-2, -2)]
HALF = jax.ShapeDtypeStruct((H, W, SHARE, B), BF)
X2C = jax.ShapeDtypeStruct((M, 4 * T), F32)


def emit(keep, send, flip, left, mask, J, i0, cube):
    for i in range(i0, i0 + cube.shape[0] // Q):
        for b in range(2):
            j = 2 * J + b
            if abs(i - j) > 4:
                continue
            q = cube[(i - i0) * Q : (i - i0 + 1) * Q, b * B : (b + 1) * B] * mask(i, j)
            x = left[pl.ds(i * Q, Q), pl.ds((J + 2) * T + b * B, B)].astype(F32)
            v = (3.0 * x - q * SCALE) * 0.5
            w = j - i + 4
            near = jnp.where(flip == 1, H - 1 - i, i)
            slot = jnp.where(flip == 1, W - 1 - w, w)
            lo, hi = v[:SHARE].astype(BF), v[SHARE:].astype(BF)
            keep[near, slot] = jnp.where(flip == 1, hi, lo)
            send[near, slot] = jnp.where(flip == 1, lo, hi)


def plus(part, i0, whole_ref, cols, j0, j1):
    n = part.shape[0] // Q
    assert j0 == i0
    total = part + whole_ref[pl.ds(i0 * Q, n * Q), cols]
    if j1 >= i0 + n:
        total = jnp.concatenate([total, whole_ref[pl.ds((i0 + n) * Q, (j1 - i0 - n + 1) * Q), cols]], axis=0)
    return total


def middle_kernel(pa, pb, xb01, mk, left, sp, xp, s1p, s1q, x2p, xh_in, sb_in, d1_in, s1_in, *outs):
    del xh_in, sb_in, d1_in, s1_in
    xh, sb, d1, s1, sdp, xc, x2c, keep, send = outs
    flip, _ = chip_share()
    mask = halo_mask(mk, pa)
    one = eye()
    unpack(pb, B_OFF, [], 0, 0, xh, one)
    xs = rows_of(xb01, xh)
    ss = square_rows(sb)

    for n, (I, J) in enumerate(S_PART):
        lo = max(I, J) - 2
        put_masked(sb_store(sb, I, J), sp[n] + nt(xs(I, lo, -3), xs(J, lo, -3)), I, J, mask)
    sb[sb_at(-2, -1)] = nt(one, ss(-1, -2, -2)).astype(BF)
    for n, (I, J) in enumerate(S_DEEP):
        sdp[n] = nt(xs(I, -2, J + 2), xs(J, -2, J + 2))
    for n, (I, J) in enumerate(D1_HALO):
        lo = max(I, J) - 2
        total = xp[n] + nt(ss(I, max(lo, -2), -1), xs(J, max(lo, -2), -1))
        if (I, J) in D1_DEEP:
            xc[D1_DEEP.index((I, J))] = total
        else:
            put_step(d1_store(d1, I, J), xs(I, J, J), total, I, J, mask)

    part = product(left, d1, 1, 0, 3, -1, -1)
    put_square(s1, plus(part, 0, s1q, pl.ds(0, T), 0, 4), 1, 0, mask)
    part = product(left, d1, 0, 0, 3, -2, -1)
    put_square(s1, plus(part, 0, s1p, pl.ds(2 * T, T), 0, 4), 0, 0, mask)

    for J in range(4, -3, -1):
        i0, i1 = in_rows(J)
        rows = pl.ds(i0 * Q, (i1 - i0 + 1) * Q)
        if J == 4:
            total = x2p[rows, pl.ds(J * T, T)]
        else:
            total = product(s1, d1, J, i0, i1, max(J - 2, 0), min(J + 2, 1))
            if J >= 0:
                total = total + x2p[rows, pl.ds(J * T, T)]
        if J >= 2:
            emit(keep, send, flip, left, mask, J, i0, total)
        else:
            x2c[rows, pl.ds((J + 2) * T, T)] = total


def middle(pa, pb, xb01, mk, left, sp, xp, s1p, s1q, x2p, xh, sb, d1, s1):
    return pl.pallas_call(
        middle_kernel,
        out_shape=[
            HROWS,
            HROWS,
            D1,
            LEFT,
            jax.ShapeDtypeStruct((len(S_DEEP), T, T), F32),
            jax.ShapeDtypeStruct((len(D1_DEEP), T, T), F32),
            X2C,
            HALF,
            HALF,
        ],
        in_specs=[VM] * 14,
        out_specs=[VM] * 9,
        input_output_aliases={10: 0, 11: 1, 12: 2, 13: 3},
        compiler_params=pltpu.CompilerParams(vmem_limit_bytes=16 * MIB),
        cost_estimate=pl.CostEstimate(flops=1000, bytes_accessed=1000, transcendentals=0),
        name="middle",
    )(pa, pb, xb01, mk, left, sp, xp, s1p, s1q, x2p, xh, sb, d1, s1)


def one_share(off, flip, mask, left, d1, s1p, x2c, sh, target):
    def rows(ref, i1, cols):
        at = [pl.multiple_of(i * Q + off, SHARE) for i in range(i1 + 1)]
        return jnp.concatenate([ref[pl.ds(a, SHARE), cols] for a in at], axis=0)

    for J in (-1, -2):
        _, i1 = in_rows(J)
        total = nn(rows(left, i1, pl.ds(0, 2 * T)), d1[J + 2, pl.ds(-J * T, 2 * T), :])
        total = total + rows(s1p, i1, pl.ds((J + 2) * T, T))
        for i in range(4):
            for b in range(2):
                j = 2 * J + b
                dst = (pl.ds(i * SHARE, SHARE), pl.ds((J + 2) * T + b * B, B))
                if abs(i - j) <= 4:
                    q = total[i * SHARE : (i + 1) * SHARE, b * B : (b + 1) * B]
                    sh[dst] = (q * mask(i, j)).astype(BF)
                else:
                    sh[dst] = jnp.zeros((SHARE, B), BF)
    for J in (1, 0, -1, -2):
        _, i1 = in_rows(J)
        last = min(i1, 3)
        k0 = max(J - 2, -2)
        a = sh[pl.ds(0, (last + 1) * SHARE), pl.ds((k0 + 2) * T, -k0 * T)]
        part = nn(a, d1[J + 2, pl.ds((k0 - J + 2) * T, -k0 * T), :])
        for i in range(i1 + 1):
            at = pl.multiple_of(i * Q + off, SHARE)
            for b in range(2):
                j = 2 * J + b
                if abs(i - j) > 4:
                    continue
                q = x2c[pl.ds(at, SHARE), pl.ds((J + 2) * T + b * B, B)]
                if i <= last:
                    q = q + part[i * SHARE : (i + 1) * SHARE, b * B : (b + 1) * B]
                x = left[pl.ds(at, SHARE), pl.ds((J + 2) * T + b * B, B)].astype(F32)
                v = (3.0 * x - q * mask(i, j) * SCALE) * 0.5
                near = jnp.where(flip == 1, H - 1 - i, i)
                slot = jnp.where(flip == 1, W - 1 - (j - i + 4), j - i + 4)
                target[near, slot] = v.astype(BF)


def finish_kernel(pa, pc, xb01, mk, left, s1p, sdp, xc, x2c, *refs):
    xh, sb, d1, send, sh = refs[4:]
    flip, _ = chip_share()
    mask = halo_mask(mk, pa)
    unpack(pc, C_OFF, C_PACK, len(C_OFF), NC * B, xh, eye())
    xs = rows_of(xb01, xh)
    ss = square_rows(sb)

    for n, (I, J) in enumerate(S_DEEP):
        lo = I - 2
        put_masked(sb_store(sb, I, J), sdp[n] + nt(xs(I, lo, -3), xs(J, lo, -3)), I, J, mask)
    for n, (I, J) in enumerate(D1_DEEP):
        lo = max(I, J) - 2
        put_step(d1_store(d1, I, J), xs(I, J, J), xc[n] + nt(ss(I, lo, -3), xs(J, lo, -3)), I, J, mask)
    one_share((1 - flip) * SHARE, flip, mask, left, d1, s1p, x2c, sh, send)


SH = pltpu.VMEM((4 * SHARE, 2 * T), BF)


def finish(pa, pc, xb01, mk, left, s1p, sdp, xc, x2c, xh, sb, d1, send):
    return pl.pallas_call(
        finish_kernel,
        out_shape=[HROWS, HROWS, D1, HALF],
        in_specs=[VM] * 13,
        out_specs=[VM] * 4,
        scratch_shapes=[SH],
        input_output_aliases={9 + n: n for n in range(4)},
        compiler_params=pltpu.CompilerParams(vmem_limit_bytes=16 * MIB),
        cost_estimate=pl.CostEstimate(flops=2 * 30 * T * T * T, bytes_accessed=4 * MIB, transcendentals=0),
        name="finish",
    )(pa, pc, xb01, mk, left, s1p, sdp, xc, x2c, xh, sb, d1, send)


def half_out(src, out, sem, first):
    copies = []
    for n in range(H):
        copies.append(pltpu.make_async_copy(src.at[n], out.at[first + n], sem.at[n]))
        copies[-1].start()
    for copy in copies:
        copy.wait()


def keep_kernel(mk, left, s1p, x2c, d1, keep_in, out, keep, sh, sem):
    del keep_in
    flip = flip_core()
    one_share(flip * SHARE, flip, own_masks(mk), left, d1, s1p, x2c, sh, keep)
    half_out(keep, out, sem, jnp.where(flip_core() == 1, H, 0))


def join_kernel(other, out_in, out, sem):
    del out_in
    half_out(other, out, sem, jnp.where(flip_core() == 1, 0, H))


OUT = jax.ShapeDtypeStruct((R, W, SHARE, B), BF)


def put_keep(mk, left, s1p, x2c, d1, keep):
    return pl.pallas_call(
        keep_kernel,
        out_shape=[OUT, HALF],
        in_specs=[VM] * 6,
        out_specs=[HBM, VM],
        scratch_shapes=[SH, pltpu.SemaphoreType.DMA((H,))],
        input_output_aliases={5: 1},
        compiler_params=pltpu.CompilerParams(vmem_limit_bytes=8 * MIB),
        cost_estimate=pl.CostEstimate(flops=1000, bytes_accessed=1000, transcendentals=0),
        name="put_keep",
    )(mk, left, s1p, x2c, d1, keep)


def join(other, out):
    return pl.pallas_call(
        join_kernel,
        out_shape=OUT,
        in_specs=[VM, HBM],
        out_specs=HBM,
        scratch_shapes=[pltpu.SemaphoreType.DMA((H,))],
        input_output_aliases={1: 0},
        compiler_params=pltpu.CompilerParams(vmem_limit_bytes=2 * MIB),
        name="join",
    )(other, out)


def chain(layers, grid):
    pairs = []
    for l in range(layers):
        for g in range(grid):
            pairs.append((l * grid + g, l * grid + (g + 1 if l % 2 == 0 else g - 1) % grid))
    return pairs


def per_device(x, ret):
    layers, grid = lax.axis_size("layer"), lax.axis_size("grid")
    cores = [(l, l ^ 1) for l in range(layers)]
    pairs = chain(layers, grid)
    x = pltpu.with_memory_space_constraint(x, pltpu.HBM)
    ret = pltpu.with_memory_space_constraint(ret, pltpu.HBM)
    pa, pb, pc, xin, mk, *outs = ahead(x, ret, pack_corner(x, ret))
    pa = lax.ppermute(pa, ("layer", "grid"), pairs)
    pb, pc, xin, mk = pack_deep(x, ret, pb, pc, xin, mk)
    pb = lax.ppermute(pb, ("layer", "grid"), pairs)
    pc = lax.ppermute(pc, ("layer", "grid"), pairs)
    xb01, xh, sb, acc, d1 = early(xin, mk, *outs)
    xh, sb, d1, swap_a, swap_b = corner(pa, xb01, acc, mk, xh, sb, d1)
    swap_a = lax.ppermute(swap_a, "layer", cores)
    swap_b = lax.ppermute(swap_b, "layer", cores)
    d1, left, sp, xp, s1p = beside(xb01, mk, xh, sb, d1)
    d1, s1, s1q, x2p = use_swapped(swap_a, swap_b, mk, left, d1)
    xh, sb, d1, s1, sdp, xc, x2c, keep, send = middle(
        pa, pb, xb01, mk, left, sp, xp, s1p, s1q, x2p, xh, sb, d1, s1
    )
    _, _, d1, send = finish(pa, pc, xb01, mk, left, s1p, sdp, xc, x2c, xh, sb, d1, send)
    other = lax.ppermute(send, "layer", cores)
    out, _ = put_keep(mk, left, s1p, x2c, d1, keep)
    return join(other, out)


def solution(mesh):
    return jax.shard_map(
        per_device,
        mesh=mesh,
        in_specs=(P("grid", None, None, None), P("grid", None)),
        out_specs=P("grid", None, "layer", None),
        check_vma=False,
    )
```
